1024 devices in a mesh: dp: 256 (over z, y_lo, x), mp: 4 (over y_hi, core).
Axes of the slice: x: 4, y: 8 (y_hi: 2, y_lo: 4; y = y_hi * 4 + y_lo), z: 16, core: 2. Of those that a mesh axis runs over, the one named last changes fastest.
Arguments:
- images: bfloat16 [32768, 1152], P('dp'), may hold values from -6 to 6
- texts: bfloat16 [32768, 1152], P('dp', 'mp'), may hold values from -6 to 6
- fc_in: bfloat16 [1152, 4304], P(None, 'mp'), may hold values from -0.1875 to 0.1875
- fc_out: bfloat16 [4304, 1152], P('mp'), may hold values from -0.09375 to 0.09375
- head: bfloat16 [1152, 1152], P('mp'), may hold values from -0.1875 to 0.1875
- partner: int32 [32768], P('dp'), may hold values from 0 to 127
Outputs:
- hidden_grad: bfloat16 [32768, 4304], P('dp', 'mp')
- text_grad: bfloat16 [32768, 1152], P('dp', 'mp')
- image_loss: float32 [32768], P('dp')
The draws below stay inside these ranges and needn't reach their ends.
All inputs are finite; a program needn't handle non-finite values.
Results may differ from the reference program's by a relative error of at most 0.024.
Values may be sent and summed in bfloat16 or wider, within the bound.
No kernel may reach another device: no remote copies, remote signals or barrier semaphores. Data moves between devices by JAX's collectives and lax.ppermute only.
A program may use at most 32 MiB of HBM per device.

```python
import jax
import jax.numpy as jnp
from jax import lax

D = 1152
FF = 4304
TOK_DEV = 128
WINDOW = 8
TOKENS = 32768
N_MP = 4


def plant(array, own_key, least, high):
    place = [jax.random.randint(jax.random.fold_in(own_key, axis), (), 0, length) for axis, length in enumerate(array.shape)]
    widest = array.shape.index(max(array.shape))
    neighbour = place[:widest] + [(place[widest] + 1) % array.shape[widest]] + place[widest + 1:]
    return array.at[tuple(place)].set(least).at[tuple(neighbour)].set(high)


def block_levels(stream_key, extent, shards, smallest, largest):
    loudness, own = 1.0, jax.random.fold_in(stream_key, 6)
    for position, shards_of in shards:
        heights = jnp.exp(jax.random.uniform(jax.random.fold_in(own, position), (shards_of,), jnp.float32, smallest / len(shards), largest / len(shards)))
        loudness = loudness * jnp.repeat(heights, extent[position] // shards_of).reshape([-1 if axis == position else 1 for axis in range(len(extent))])
    return loudness


def normal_values(own_key, extent, scale, reach, split=(), held_as=jnp.bfloat16):
    level = block_levels(own_key, extent, split, -0.22, 0.18) if split else 1.0
    result = jax.random.normal(own_key, extent, jnp.float32) * scale * level
    return jnp.minimum(jnp.maximum(result, -reach), reach).astype(held_as)


def setup_inputs(seed: int = 0) -> dict:
    arg_keys = jax.random.split(jax.random.key(seed), 7)
    images = normal_values(arg_keys[0], (TOKENS, D), 1.0, 6.0, ((0, 256),))
    texts = normal_values(arg_keys[1], (TOKENS, D), 1.0, 6.0, ((0, 256), (1, 4)))
    fc_in = normal_values(arg_keys[2], (D, FF), D ** -0.5, 0.1875, ((1, 4),))
    fc_out = normal_values(arg_keys[3], (FF, D), FF ** -0.5, 0.09375, ((0, 4),))
    head = normal_values(arg_keys[4], (D, D), D ** -0.5, 0.1875, ((0, 4),))
    partner = plant(jax.random.randint(arg_keys[5], (TOKENS,), 0, TOK_DEV), jax.random.fold_in(arg_keys[5], 1), 0, TOK_DEV - 1).astype(jnp.int32)
    return dict(images=images, texts=texts, fc_in=fc_in, fc_out=fc_out, head=head, partner=partner)


logit_scale = 32.0
logit_bias = -2.0
loss_scale = 16.0
epsilon = 1e-06

def grouped_sum(left, right):
    width = left.shape[1] // N_MP
    total = jnp.zeros((left.shape[0], right.shape[1]), jnp.float32)
    for group in range(N_MP):
        piece = jnp.dot(left[:, group * width:(group + 1) * width], right[group * width:(group + 1) * width], preferred_element_type=jnp.float32)
        total = total + piece.astype(jnp.bfloat16).astype(jnp.float32)
    return total

def unit_rows(embed):
    inverse = lax.rsqrt(lax.optimization_barrier(jnp.sum(embed * embed, axis=1, keepdims=True)) + epsilon)
    return (embed * inverse, inverse)

def reference(images, texts, fc_in, fc_out, head, partner):
    block_count = TOKENS // TOK_DEV
    pre_act = jnp.dot(images, fc_in, preferred_element_type=jnp.float32)
    activation = jax.nn.gelu(pre_act, approximate=True).astype(jnp.bfloat16)
    image_emb = images.astype(jnp.float32) + grouped_sum(activation, fc_out)
    text_emb = grouped_sum(texts, head)
    image_unit, image_inv = unit_rows(image_emb)
    text_unit, text_inv = unit_rows(text_emb)
    img_blocks = image_unit.reshape(block_count, TOK_DEV, D)
    txt_blocks = text_unit.reshape(block_count, TOK_DEV, D)
    columns = jnp.arange(TOK_DEV, dtype=jnp.int32)
    positive = columns[None, None, :] == partner.reshape(block_count, TOK_DEV)[:, :, None]
    loss_total = jnp.zeros((block_count, TOK_DEV), jnp.float32)
    unit_grad = jnp.zeros_like(img_blocks)
    text_unit_grad = jnp.zeros_like(txt_blocks)
    for offset in range(WINDOW):
        visiting = jnp.roll(txt_blocks, offset, axis=0)
        logits = logit_scale * jnp.einsum('bid,bjd->bij', img_blocks, visiting, precision=lax.Precision.HIGHEST) + logit_bias
        if offset == 0:
            label_sign = jnp.where(positive, 1.0, -1.0).astype(jnp.float32)
        else:
            label_sign = jnp.full(logits.shape, -1.0, jnp.float32)
        flipped = -label_sign * logits
        loss_total = loss_total + lax.optimization_barrier(jnp.sum(jax.nn.softplus(flipped), axis=2))
        pair_grad = -loss_scale * label_sign * jax.nn.sigmoid(flipped)
        unit_grad = unit_grad + logit_scale * jnp.einsum('bij,bjd->bid', pair_grad, visiting, precision=lax.Precision.HIGHEST)
        back_terms = logit_scale * jnp.einsum('bij,bid->bjd', pair_grad, img_blocks, precision=lax.Precision.HIGHEST)
        text_unit_grad = text_unit_grad + jnp.roll(back_terms, -offset, axis=0)
    unit_grad = unit_grad.reshape(TOKENS, D)
    text_unit_grad = text_unit_grad.reshape(TOKENS, D)
    image_emb_grad = ((unit_grad - image_unit * lax.optimization_barrier(jnp.sum(image_unit * unit_grad, axis=1, keepdims=True))) * image_inv).astype(jnp.bfloat16)
    text_emb_grad = ((text_unit_grad - text_unit * lax.optimization_barrier(jnp.sum(text_unit * text_unit_grad, axis=1, keepdims=True))) * text_inv).astype(jnp.bfloat16)
    act_grad = jnp.dot(image_emb_grad, fc_out.T, preferred_element_type=jnp.float32)
    unused, pullback = jax.vjp(lambda value: jax.nn.gelu(value, approximate=True), pre_act)
    hidden_grad = pullback(act_grad)[0].astype(jnp.bfloat16)
    text_grad = jnp.dot(text_emb_grad, head.T, preferred_element_type=jnp.float32).astype(jnp.bfloat16)
    image_loss = loss_total.reshape(TOKENS) / (WINDOW * TOK_DEV)
    return (hidden_grad, text_grad, image_loss)
```

```python
import jax
import jax.numpy as jnp
from jax import lax
from jax.sharding import Mesh, PartitionSpec as P

WINDOW = 8


logit_scale = 32.0
logit_bias = -2.0
loss_scale = 16.0
epsilon = 1e-06

AXES = ("z", "y_lo", "x", "y_hi", "core")
SIZES = (16, 4, 4, 2, 2)
MP = ("y_hi", "core")
NEAR = 4


def place(block, role):
    z = block // 16
    y_hi = (role // 2) ^ (z & 1)
    return block * 4 + y_hi * 2 + role % 2


def moves(shift):
    return [
        (place(block, role), place((block + shift(role)) % 256, role))
        for block in range(256)
        for role in range(4)
    ]


def move(value, shift):
    return lax.ppermute(value, AXES, moves(shift))


def unit_rows(embed):
    inverse = lax.rsqrt(jnp.sum(embed * embed, axis=1, keepdims=True) + epsilon)
    return (embed * inverse, inverse)


def tangent_rows(grad, unit, inverse):
    return ((grad - unit * jnp.sum(unit * grad, axis=1, keepdims=True)) * inverse).astype(
        jnp.bfloat16
    )


def core_sum(term):
    halves = term.astype(jnp.bfloat16).reshape(2, term.shape[0] // 2, term.shape[1])
    got = lax.all_to_all(halves, "core", 0, 0).astype(jnp.float32)
    return (got[0] + got[1]).astype(jnp.bfloat16)


def chip_sum(gathered):
    both = gathered[:2].astype(jnp.float32) + gathered[2:].astype(jnp.float32)
    return both.reshape(both.shape[0] * both.shape[1], both.shape[2])


def local(images, texts, fc_in, fc_out, head, partner):
    rows, width = images.shape
    shift = 2 * (lax.axis_index("y_hi") ^ (lax.axis_index("z") & 1)) + lax.axis_index("core")

    text_term = jnp.dot(texts, head, preferred_element_type=jnp.float32)
    pre_act = jnp.dot(images, fc_in, preferred_element_type=jnp.float32)
    activation = jax.nn.gelu(pre_act, approximate=True).astype(jnp.bfloat16)
    image_term = jnp.dot(activation, fc_out, preferred_element_type=jnp.float32)

    text_emb = chip_sum(lax.all_gather(core_sum(text_term), MP))
    text_unit, text_inv = unit_rows(text_emb)
    text_own = text_unit.astype(jnp.bfloat16)
    text_far = move(text_own, lambda role: NEAR)
    image_emb = images.astype(jnp.float32) + chip_sum(lax.all_gather(core_sum(image_term), MP))
    image_unit, image_inv = unit_rows(image_emb)
    scored = move(image_unit.astype(jnp.bfloat16), lambda role: -role)
    visiting = jnp.concatenate([text_own, text_far], 0)

    logits = (
        logit_scale
        * lax.dot_general(
            scored, visiting, (((1,), (1,)), ((), ())), preferred_element_type=jnp.float32
        )
        + logit_bias
    )
    columns = lax.broadcasted_iota(jnp.int32, logits.shape, 1)
    positive = (columns == partner[:, None]) & (shift == 0)
    label_sign = jnp.where(positive, 1.0, -1.0).astype(jnp.float32)
    flipped = -label_sign * logits
    loss_part = jnp.sum(jax.nn.softplus(flipped), axis=1, keepdims=True)
    pair_grad = (-loss_scale * label_sign * jax.nn.sigmoid(flipped)).astype(jnp.bfloat16)
    image_part = logit_scale * jnp.dot(pair_grad, visiting, preferred_element_type=jnp.float32)
    text_part = logit_scale * lax.dot_general(
        pair_grad, scored, (((0,), (0,)), ((), ())), preferred_element_type=jnp.float32
    )

    loss_high = loss_part.astype(jnp.bfloat16)
    loss_low = (loss_part - loss_high.astype(jnp.float32)).astype(jnp.bfloat16)
    lanes = lax.broadcasted_iota(jnp.int32, (rows, 128), 1)
    loss_lanes = jnp.where(lanes == 0, loss_high, jnp.where(lanes == 1, loss_low, 0))
    image_sent = jnp.concatenate([image_part.astype(jnp.bfloat16), loss_lanes], 1)
    image_back = move(image_sent, lambda role: role)
    text_back = move(text_part[rows:].astype(jnp.bfloat16), lambda role: -NEAR)
    text_total = text_part[:rows] + text_back.astype(jnp.float32)

    image_half = core_sum(image_back.astype(jnp.float32))
    text_half = core_sum(text_total)
    image_sums, text_sums = lax.all_gather((image_half, text_half), MP)
    image_all = chip_sum(image_sums)
    loss_all = image_all[:, width] + image_all[:, width + 1]
    image_emb_grad = tangent_rows(image_all[:, :width], image_unit, image_inv)
    text_emb_grad = tangent_rows(chip_sum(text_sums), text_unit, text_inv)

    act_grad = lax.dot_general(
        image_emb_grad, fc_out, (((1,), (1,)), ((), ())), preferred_element_type=jnp.float32
    )
    unused, pullback = jax.vjp(lambda value: jax.nn.gelu(value, approximate=True), pre_act)
    hidden_grad = pullback(act_grad)[0].astype(jnp.bfloat16)
    text_grad = lax.dot_general(
        text_emb_grad, head, (((1,), (1,)), ((), ())), preferred_element_type=jnp.float32
    ).astype(jnp.bfloat16)
    image_loss = loss_all / (WINDOW * rows)
    return (hidden_grad, text_grad, image_loss)


def solution(mesh):
    dp = ("z", "y_lo", "x")
    return jax.shard_map(
        local,
        mesh=Mesh(mesh.devices.reshape(SIZES), AXES),
        in_specs=(P(dp, None), P(dp, MP), P(None, MP), P(MP, None), P(MP, None), P(dp)),
        out_specs=(P(dp, MP), P(dp, MP), P(dp)),
        check_vma=False,
    )
```

```python
import jax
import jax.numpy as jnp
from jax import lax
from jax.sharding import Mesh, PartitionSpec as P

WINDOW = 8


logit_scale = 32.0
logit_bias = -2.0
loss_scale = 16.0
epsilon = 1e-06

AXES = ("z", "y_lo", "x", "y_hi", "core")
SIZES = (16, 4, 4, 2, 2)
MP = ("y_hi", "core")
NEAR = 4


def place(block, role):
    z = block // 16
    y_hi = (role // 2) ^ (z & 1)
    return block * 4 + y_hi * 2 + role % 2


def moves(shift):
    return [
        (place(block, role), place((block + shift(role)) % 256, role))
        for block in range(256)
        for role in range(4)
    ]


def move(value, shift):
    return lax.ppermute(value, AXES, moves(shift))


def unit_rows(embed):
    inverse = lax.rsqrt(jnp.sum(embed * embed, axis=1, keepdims=True) + epsilon)
    return (embed * inverse, inverse)


def tangent_rows(grad, unit, inverse):
    return ((grad - unit * jnp.sum(unit * grad, axis=1, keepdims=True)) * inverse).astype(
        jnp.bfloat16
    )


def core_halves(term, core):
    half = term.shape[0] // 2
    return (
        lax.dynamic_slice_in_dim(term, core * half, half, 0),
        lax.dynamic_slice_in_dim(term, (1 - core) * half, half, 0),
    )


def reduced(image_term, text_term, core):
    halves = [core_halves(term, core) for term in (image_term, text_term)]
    kept = jnp.concatenate([half[0] for half in halves], 0)
    sent = jnp.concatenate([half[1].astype(jnp.bfloat16) for half in halves], 0)
    got = lax.ppermute(sent, "core", [(0, 1), (1, 0)])
    chip = (kept.astype(jnp.float32) + got.astype(jnp.float32)).astype(jnp.bfloat16)
    both = lax.all_gather(chip, "y_hi").astype(jnp.float32)
    return both[0] + both[1]


def core_gather(image_half, text_half):
    half = image_half.shape[0]
    both = lax.all_gather(jnp.concatenate([image_half, text_half], 0), "core")
    return both[:, :half].reshape(2 * half, -1), both[:, half:].reshape(2 * half, -1)


def split_loss(loss):
    high = loss.astype(jnp.bfloat16)
    low = (loss - high.astype(jnp.float32)).astype(jnp.bfloat16)
    lanes = lax.broadcasted_iota(jnp.int32, (loss.shape[0], 128), 1)
    return jnp.where(lanes == 0, high, jnp.where(lanes == 1, low, 0)).astype(jnp.bfloat16)


def local(images, texts, fc_in, fc_out, head, partner):
    rows, width = images.shape
    half = rows // 2
    core = lax.axis_index("core")
    shift = 2 * (lax.axis_index("y_hi") ^ (lax.axis_index("z") & 1)) + core

    text_term = jnp.dot(texts, head, preferred_element_type=jnp.float32)
    pre_act = jnp.dot(images, fc_in, preferred_element_type=jnp.float32)
    activation = jax.nn.gelu(pre_act, approximate=True).astype(jnp.bfloat16)
    image_term = jnp.dot(activation, fc_out, preferred_element_type=jnp.float32)

    sums = reduced(image_term, text_term, core)
    image_emb = core_halves(images, core)[0].astype(jnp.float32) + sums[:half]
    image_unit, image_inv = unit_rows(image_emb)
    text_unit, text_inv = unit_rows(sums[half:])
    image_own, text_own = core_gather(image_unit.astype(jnp.bfloat16), text_unit.astype(jnp.bfloat16))
    scored = move(image_own, lambda role: -role)
    text_far = move(text_own, lambda role: NEAR)
    visiting = jnp.concatenate([text_own, text_far], 0)

    logits = (
        logit_scale
        * lax.dot_general(
            scored, visiting, (((1,), (1,)), ((), ())), preferred_element_type=jnp.float32
        )
        + logit_bias
    )
    columns = lax.broadcasted_iota(jnp.int32, logits.shape, 1)
    positive = (columns == partner[:, None]) & (shift == 0)
    label_sign = jnp.where(positive, 1.0, -1.0).astype(jnp.float32)
    flipped = -label_sign * logits
    loss_part = jnp.sum(jax.nn.softplus(flipped), axis=1, keepdims=True)
    pair_grad = (-loss_scale * label_sign * jax.nn.sigmoid(flipped)).astype(jnp.bfloat16)
    image_part = logit_scale * jnp.dot(pair_grad, visiting, preferred_element_type=jnp.float32)
    text_part = logit_scale * lax.dot_general(
        pair_grad, scored, (((0,), (0,)), ((), ())), preferred_element_type=jnp.float32
    )

    image_sent = jnp.concatenate([image_part.astype(jnp.bfloat16), split_loss(loss_part)], 1)
    image_back = move(image_sent, lambda role: role)
    text_back = move(text_part[rows:].astype(jnp.bfloat16), lambda role: -NEAR)
    text_total = text_part[:rows] + text_back.astype(jnp.float32)

    sums = reduced(image_back, jnp.pad(text_total, ((0, 0), (0, 128))), core)
    loss_half = sums[:half, width : width + 1] + sums[:half, width + 1 : width + 2]
    image_half = tangent_rows(sums[:half, :width], image_unit, image_inv)
    text_half = tangent_rows(sums[half:, :width], text_unit, text_inv)
    image_emb_grad, text_emb_grad = core_gather(
        jnp.concatenate([image_half, split_loss(loss_half)], 1),
        jnp.pad(text_half, ((0, 0), (0, 128))),
    )
    loss_all = image_emb_grad[:, width : width + 2].astype(jnp.float32).sum(axis=1)
    image_emb_grad, text_emb_grad = image_emb_grad[:, :width], text_emb_grad[:, :width]

    act_grad = lax.dot_general(
        image_emb_grad, fc_out, (((1,), (1,)), ((), ())), preferred_element_type=jnp.float32
    )
    unused, pullback = jax.vjp(lambda value: jax.nn.gelu(value, approximate=True), pre_act)
    hidden_grad = pullback(act_grad)[0].astype(jnp.bfloat16)
    text_grad = lax.dot_general(
        text_emb_grad, head, (((1,), (1,)), ((), ())), preferred_element_type=jnp.float32
    ).astype(jnp.bfloat16)
    image_loss = loss_all / (WINDOW * rows)
    return (hidden_grad, text_grad, image_loss)


def solution(mesh):
    dp = ("z", "y_lo", "x")
    return jax.shard_map(
        local,
        mesh=Mesh(mesh.devices.reshape(SIZES), AXES),
        in_specs=(P(dp, None), P(dp, MP), P(None, MP), P(MP, None), P(MP, None), P(dp)),
        out_specs=(P(dp, MP), P(dp, MP), P(dp)),
        check_vma=False,
    )
```

```python
import jax
import jax.numpy as jnp
from jax import lax
from jax.sharding import Mesh, PartitionSpec as P

WINDOW = 8


logit_scale = 32.0
logit_bias = -2.0
loss_scale = 16.0
epsilon = 1e-06

AXES = ("z", "y_lo", "x", "y_hi", "core")
SIZES = (16, 4, 4, 2, 2)
MP = ("y_hi", "core")
NEAR = 4
OFFSET = (0, 3, 1, 2)


def place(block, role):
    z = block // 16
    y_hi = (role // 2) ^ (z & 1)
    return block * 4 + y_hi * 2 + role % 2


def moves(shift):
    return [
        (place(block, role), place((block + shift(role)) % 256, role))
        for block in range(256)
        for role in range(4)
    ]


def move(value, shift):
    return lax.ppermute(value, AXES, moves(shift))


def unit_rows(embed):
    inverse = lax.rsqrt(jnp.sum(embed * embed, axis=1, keepdims=True) + epsilon)
    return (embed * inverse, inverse)


def tangent_rows(grad, unit, inverse):
    return ((grad - unit * jnp.sum(unit * grad, axis=1, keepdims=True)) * inverse).astype(
        jnp.bfloat16
    )


def core_halves(term, core):
    half = term.shape[0] // 2
    return (
        lax.dynamic_slice_in_dim(term, core * half, half, 0),
        lax.dynamic_slice_in_dim(term, (1 - core) * half, half, 0),
    )


def reduced(image_term, text_term, core):
    halves = [core_halves(term, core) for term in (image_term, text_term)]
    kept = jnp.concatenate([half[0] for half in halves], 0)
    sent = jnp.concatenate([half[1].astype(jnp.bfloat16) for half in halves], 0)
    got = lax.ppermute(sent, "core", [(0, 1), (1, 0)])
    chip = (kept.astype(jnp.float32) + got.astype(jnp.float32)).astype(jnp.bfloat16)
    both = lax.all_gather(chip, "y_hi").astype(jnp.float32)
    return both[0] + both[1]


def core_gather(image_half, text_half):
    half = image_half.shape[0]
    both = lax.all_gather(jnp.concatenate([image_half, text_half], 0), "core")
    return both[:, :half].reshape(2 * half, -1), both[:, half:].reshape(2 * half, -1)


def split_loss(loss):
    high = loss.astype(jnp.bfloat16)
    low = (loss - high.astype(jnp.float32)).astype(jnp.bfloat16)
    lanes = lax.broadcasted_iota(jnp.int32, (loss.shape[0], 128), 1)
    return jnp.where(lanes == 0, high, jnp.where(lanes == 1, low, 0)).astype(jnp.bfloat16)


def scored(own, others, positive):
    logits = (
        logit_scale
        * lax.dot_general(
            own, others, (((1,), (1,)), ((), ())), preferred_element_type=jnp.float32
        )
        + logit_bias
    )
    label_sign = jnp.where(positive, 1.0, -1.0).astype(jnp.float32)
    flipped = -label_sign * logits
    loss = jnp.sum(jax.nn.softplus(flipped), axis=1, keepdims=True)
    pair_grad = (-loss_scale * label_sign * jax.nn.sigmoid(flipped)).astype(jnp.bfloat16)
    return logit_scale * jnp.dot(pair_grad, others, preferred_element_type=jnp.float32), loss


def local(images, texts, fc_in, fc_out, head, partner):
    rows, width = images.shape
    half = rows // 2
    core = lax.axis_index("core")
    role = 2 * (lax.axis_index("y_hi") ^ (lax.axis_index("z") & 1)) + core

    text_term = jnp.dot(texts, head, preferred_element_type=jnp.float32)
    pre_act = jnp.dot(images, fc_in, preferred_element_type=jnp.float32)
    activation = jax.nn.gelu(pre_act, approximate=True).astype(jnp.bfloat16)
    image_term = jnp.dot(activation, fc_out, preferred_element_type=jnp.float32)

    sums = reduced(image_term, text_term, core)
    image_emb = core_halves(images, core)[0].astype(jnp.float32) + sums[:half]
    image_unit, image_inv = unit_rows(image_emb)
    text_unit, text_inv = unit_rows(sums[half:])
    image_own, text_own = core_gather(image_unit.astype(jnp.bfloat16), text_unit.astype(jnp.bfloat16))
    visits = (
        move(text_own, lambda role: OFFSET[role] + NEAR),
        move(image_own, lambda role: -OFFSET[role] - NEAR),
        move(text_own, lambda role: OFFSET[role]),
        move(image_own, lambda role: -OFFSET[role]),
    )
    paired = jnp.where(role == 0, partner, -1)
    columns = lax.broadcasted_iota(jnp.int32, (rows, 2 * rows), 1)
    on_row = lax.broadcasted_iota(jnp.int32, (rows, 2 * rows), 0)
    image_part, loss_part = scored(
        image_own, jnp.concatenate([visits[2], visits[0]], 0), columns == paired[:, None]
    )
    text_part, unused = scored(
        text_own,
        jnp.concatenate([visits[3], visits[1]], 0),
        on_row == jnp.pad(paired, (0, rows), constant_values=-1)[None, :],
    )

    image_part = jnp.concatenate([image_part, split_loss(loss_part).astype(jnp.float32)], 1)
    sums = reduced(image_part, jnp.pad(text_part, ((0, 0), (0, 128))), core)
    loss_half = sums[:half, width : width + 1] + sums[:half, width + 1 : width + 2]
    image_half = tangent_rows(sums[:half, :width], image_unit, image_inv)
    text_half = tangent_rows(sums[half:, :width], text_unit, text_inv)
    image_emb_grad, text_emb_grad = core_gather(
        jnp.concatenate([image_half, split_loss(loss_half)], 1),
        jnp.pad(text_half, ((0, 0), (0, 128))),
    )
    loss_all = image_emb_grad[:, width : width + 2].astype(jnp.float32).sum(axis=1)
    image_emb_grad, text_emb_grad = image_emb_grad[:, :width], text_emb_grad[:, :width]

    act_grad = lax.dot_general(
        image_emb_grad, fc_out, (((1,), (1,)), ((), ())), preferred_element_type=jnp.float32
    )
    unused, pullback = jax.vjp(lambda value: jax.nn.gelu(value, approximate=True), pre_act)
    hidden_grad = pullback(act_grad)[0].astype(jnp.bfloat16)
    text_grad = lax.dot_general(
        text_emb_grad, head, (((1,), (1,)), ((), ())), preferred_element_type=jnp.float32
    ).astype(jnp.bfloat16)
    image_loss = loss_all / (WINDOW * rows)
    return (hidden_grad, text_grad, image_loss)


def solution(mesh):
    dp = ("z", "y_lo", "x")
    return jax.shard_map(
        local,
        mesh=Mesh(mesh.devices.reshape(SIZES), AXES),
        in_specs=(P(dp, None), P(dp, MP), P(None, MP), P(MP, None), P(MP, None), P(dp)),
        out_specs=(P(dp, MP), P(dp, MP), P(dp)),
        check_vma=False,
    )
```

```python
import jax
import jax.numpy as jnp
from jax import lax
from jax.experimental import pallas as pl
from jax.experimental.pallas import tpu as pltpu
from jax.sharding import Mesh, PartitionSpec as P

WINDOW = 8


logit_scale = 32.0
logit_bias = -2.0
loss_scale = 16.0
epsilon = 1e-06

AXES = ("z", "y_lo", "x", "y_hi", "core")
SIZES = (16, 4, 4, 2, 2)
MP = ("y_hi", "core")
NEAR = 4
OFFSET = (0, 3, 1, 2)
HALF = 64
LANES = 128
GELU_SCALE = 0.7978845608028654
GELU_CUBIC = 0.044715


def place(block, role):
    z = block // 16
    y_hi = (role // 2) ^ (z & 1)
    return block * 4 + y_hi * 2 + role % 2


def moves(shift):
    return [
        (place(block, role), place((block + shift(role)) % 256, role))
        for block in range(256)
        for role in range(4)
    ]


def move(value, shift):
    return lax.ppermute(value, AXES, moves(shift))


def dot(left, right, left_dim, right_dim):
    return lax.dot_general(
        left, right, (((left_dim,), (right_dim,)), ((), ())), preferred_element_type=jnp.float32
    )


def own_half(array, core):
    return array[pl.ds(pl.multiple_of(core * HALF, HALF), HALF), :]


def heads_kernel(
    core_ref, images_ref, texts_ref, fc_in_ref, fc_out_ref, head_ref,
    slope_ref, kept_ref, sent_ref, image_term, text_term,
):
    core = core_ref[0]
    text_term[...] = dot(texts_ref[...], head_ref[...], 0, 0)
    pre_act = dot(fc_in_ref[...], images_ref[...], 1, 1)
    square = pre_act * pre_act
    bent = jnp.tanh(GELU_SCALE * pre_act * (1.0 + GELU_CUBIC * square))
    activation = (0.5 * pre_act * (1.0 + bent)).astype(jnp.bfloat16)
    slope_ref[...] = 0.5 * (1.0 + bent) + (
        0.5 * GELU_SCALE * pre_act * (1.0 - bent * bent) * (1.0 + 3.0 * GELU_CUBIC * square)
    )
    image_term[...] = dot(activation, fc_out_ref[...], 0, 0)
    for first, term in ((0, image_term), (HALF, text_term)):
        kept_ref[first : first + HALF] = own_half(term, core)
        sent_ref[first : first + HALF] = own_half(term, 1 - core).astype(jnp.bfloat16)


def unit_kernel(core_ref, chips_ref, images_ref, unit_ref, inverse_ref, sent_ref):
    embed = chips_ref[0].astype(jnp.float32) + chips_ref[1].astype(jnp.float32)
    image_embed = own_half(images_ref, core_ref[0]).astype(jnp.float32) + embed[:HALF]
    for first, rows in ((0, image_embed), (HALF, embed[HALF:])):
        inverse = lax.rsqrt(jnp.sum(rows * rows, axis=1, keepdims=True) + epsilon)
        unit = rows * inverse
        unit_ref[first : first + HALF] = unit
        inverse_ref[first : first + HALF] = jnp.broadcast_to(inverse, (HALF, LANES))
        sent_ref[first : first + HALF] = unit.astype(jnp.bfloat16)


def split_loss(loss):
    high = loss.astype(jnp.bfloat16).astype(jnp.float32)
    lanes = lax.broadcasted_iota(jnp.int32, (loss.shape[0], LANES), 1)
    return jnp.where(lanes == 0, high, jnp.where(lanes == 1, loss - high, 0.0))


def pair_terms(own, others, positive):
    logits = logit_scale * dot(own, others, 1, 1) + logit_bias
    if positive is None:
        flipped = logits
    else:
        flipped = jnp.where(positive, -logits, logits)
    small = jnp.exp(-jnp.abs(flipped))
    loss = jnp.maximum(flipped, 0.0) + jnp.log1p(small)
    sigmoid = jnp.where(flipped >= 0.0, 1.0, small) / (1.0 + small)
    if positive is None:
        pair_grad = loss_scale * sigmoid
    else:
        pair_grad = jnp.where(positive, -loss_scale, loss_scale) * sigmoid
    return logit_scale * dot(pair_grad.astype(jnp.bfloat16), others, 1, 0), loss


def score_kernel(
    core_ref, image_ref, text_ref, near_text_ref, far_text_ref, near_image_ref, far_image_ref,
    column_ref, row_ref, kept_ref, sent_ref, image_part, text_part,
):
    core = core_ref[0]
    rows, width = image_ref.shape
    across = lax.broadcasted_iota(jnp.int32, (rows, rows), 1)
    down = lax.broadcasted_iota(jnp.int32, (rows, rows), 0)
    near, near_loss = pair_terms(image_ref[...], near_text_ref[...], across == column_ref[...])
    far, far_loss = pair_terms(image_ref[...], far_text_ref[...], None)
    image_part[:, :width] = near + far
    image_part[:, width:] = split_loss(jnp.sum(near_loss + far_loss, axis=1, keepdims=True))
    near, unused = pair_terms(text_ref[...], near_image_ref[...], down == row_ref[...])
    far, unused = pair_terms(text_ref[...], far_image_ref[...], None)
    text_part[:, :width] = near + far
    text_part[:, width:] = jnp.zeros((rows, LANES), jnp.float32)
    for first, part in ((0, image_part), (HALF, text_part)):
        kept_ref[first : first + HALF] = own_half(part, core)
        sent_ref[first : first + HALF] = own_half(part, 1 - core).astype(jnp.bfloat16)


def tangent_kernel(chips_ref, unit_ref, inverse_ref, sent_ref):
    width = unit_ref.shape[1]
    sums = chips_ref[0].astype(jnp.float32) + chips_ref[1].astype(jnp.float32)
    grad, unit = sums[:, :width], unit_ref[...]
    along = jnp.sum(unit * grad, axis=1, keepdims=True)
    tangent = (grad - unit * along) * inverse_ref[:, :1]
    sent_ref[:, :width] = tangent.astype(jnp.bfloat16)
    loss = sums[:, width : width + 1] + sums[:, width + 1 : width + 2]
    sent_ref[:, width:] = split_loss(loss).astype(jnp.bfloat16)


def backward_kernel(
    grads_ref, slope_ref, fc_out_ref, head_ref, hidden_ref, text_ref, loss_ref
):
    rows, width = 2 * HALF, fc_out_ref.shape[1]
    image_grad = grads_ref[:, :HALF].reshape(rows, width + LANES)
    text_grad = grads_ref[:, HALF:].reshape(rows, width + LANES)
    losses = jnp.sum(image_grad[:, width:].astype(jnp.float32), axis=1, keepdims=True)
    loss_ref[...] = jnp.broadcast_to(losses, (rows, LANES)).T / (WINDOW * rows)
    act_grad = dot(fc_out_ref[...], image_grad[:, :width], 1, 1)
    hidden_ref[...] = (slope_ref[...] * act_grad).astype(jnp.bfloat16)
    text_ref[...] = dot(head_ref[...], text_grad[:, :width], 1, 1).astype(jnp.bfloat16)


def kernel(body, outs, scratch=(), places=""):
    spaces = dict(s=pltpu.SMEM, v=pltpu.VMEM)
    return pl.pallas_call(
        body,
        out_shape=[jax.ShapeDtypeStruct(shape, dtype) for shape, dtype in outs],
        in_specs=[pl.BlockSpec(memory_space=spaces[place]) for place in places],
        out_specs=[pl.BlockSpec(memory_space=pltpu.VMEM) for unused in outs],
        scratch_shapes=list(scratch),
        compiler_params=pltpu.CompilerParams(vmem_limit_bytes=24 * 1024 * 1024),
    )


def chip_gather(kept, sent):
    got = lax.ppermute(sent, "core", [(0, 1), (1, 0)])
    return lax.all_gather((kept + got.astype(jnp.float32)).astype(jnp.bfloat16), "y_hi")


def local(images, texts, fc_in, fc_out, head, partner):
    rows, width = images.shape
    hidden, features = fc_out.shape[0], head.shape[0]
    f32, bf16 = jnp.float32, jnp.bfloat16
    core = lax.axis_index("core")
    role = 2 * (lax.axis_index("y_hi") ^ (lax.axis_index("z") & 1)) + core
    core = core.reshape(1)

    slope, kept, sent = kernel(
        heads_kernel,
        [((hidden, rows), f32), ((rows, width), f32), ((rows, width), bf16)],
        [
            pltpu.VMEM((rows, width), f32),
            pltpu.VMEM((rows, width), f32),
        ],
        "svvvvv",
    )(core, images, texts.T, fc_in.T, fc_out, head)

    unit, inverse, unit_sent = kernel(
        unit_kernel,
        [((rows, width), f32), ((rows, LANES), f32), ((rows, width), bf16)],
        places="svv",
    )(core, chip_gather(kept, sent), images)

    units = lax.all_gather(unit_sent, "core")
    image_own = units[:, :HALF].reshape(rows, width)
    text_own = units[:, HALF:].reshape(rows, width)
    far_text = move(text_own, lambda role: OFFSET[role] + NEAR)
    far_image = move(image_own, lambda role: -OFFSET[role] - NEAR)
    near_text = move(text_own, lambda role: OFFSET[role])
    near_image = move(image_own, lambda role: -OFFSET[role])

    paired = jnp.where(role == 0, partner, -1)
    columns = width + LANES
    kept, sent = kernel(
        score_kernel,
        [((rows, columns), f32), ((rows, columns), bf16)],
        [pltpu.VMEM((rows, columns), f32), pltpu.VMEM((rows, columns), f32)],
        "svvvvvvvv",
    )(
        core, image_own, text_own, near_text, far_text, near_image, far_image,
        paired.reshape(rows, 1), paired.reshape(1, rows),
    )

    (grads,) = kernel(tangent_kernel, [((rows, columns), bf16)], places="vvv")(
        chip_gather(kept, sent), unit, inverse
    )
    hidden_grad, text_grad, loss = kernel(
        backward_kernel,
        [((hidden, rows), bf16), ((features, rows), bf16), ((rows, rows), f32)],
        places="vvvv",
    )(lax.all_gather(grads, "core"), slope, fc_out, head)
    return (hidden_grad.T, text_grad.T, loss[0])


def solution(mesh):
    dp = ("z", "y_lo", "x")
    return jax.shard_map(
        local,
        mesh=Mesh(mesh.devices.reshape(SIZES), AXES),
        in_specs=(P(dp, None), P(dp, MP), P(None, MP), P(MP, None), P(MP, None), P(dp)),
        out_specs=(P(dp, MP), P(dp, MP), P(dp)),
        check_vma=False,
    )
```

```python
import jax
import jax.numpy as jnp
from jax import lax
from jax.experimental import pallas as pl
from jax.experimental.pallas import tpu as pltpu
from jax.sharding import Mesh, PartitionSpec as P

WINDOW = 8


logit_scale = 32.0
logit_bias = -2.0
loss_scale = 16.0
epsilon = 1e-06

AXES = ("z", "y_lo", "x", "y_hi", "core")
SIZES = (16, 4, 4, 2, 2)
MP = ("y_hi", "core")
NEAR = 4
OFFSET = (0, 2, 1, 3)
HALF = 64
LANES = 128
HEADS_VMEM = 56
CUTS = 3
GELU_SCALE = 0.7978845608028654
GELU_CUBIC = 0.044715


def place(block, role):
    z = block // 16
    y_hi = (role // 2) ^ (z & 1)
    return block * 4 + y_hi * 2 + role % 2


def moves(shift):
    return [
        (place(block, role), place((block + shift(role)) % 256, role))
        for block in range(256)
        for role in range(4)
    ]


def move(value, shift):
    return lax.ppermute(value, AXES, moves(shift))


def dot(left, right, left_dim, right_dim):
    return lax.dot_general(
        left, right, (((left_dim,), (right_dim,)), ((), ())), preferred_element_type=jnp.float32
    )


def own_half(array, core):
    return array[pl.ds(pl.multiple_of(core * HALF, HALF), HALF), :]


def heads_kernel(
    core_ref, texts_hbm, head_hbm, images_hbm, fc_in_hbm, fc_out_hbm,
    slope_ref, kept_ref, sent_ref,
    texts_ref, head_ref, images_ref, fc_in_ref, fc_out_ref, image_term, text_term, sems,
):
    core = core_ref[0]
    width = images_ref.shape[1]
    cuts = [pl.ds(first, width // CUTS) for first in range(0, width, width // CUTS)]
    pairs = [(texts_hbm, texts_ref), (head_hbm, head_ref), (images_hbm, images_ref)]
    for source, target in ((fc_in_hbm, fc_in_ref), (fc_out_hbm, fc_out_ref)):
        pairs += [(source.at[:, cut], target.at[:, cut]) for cut in cuts]
    copies = [
        pltpu.make_async_copy(source, target, sems.at[index])
        for index, (source, target) in enumerate(pairs)
    ]
    for copy in copies:
        copy.start()
    for copy in copies[:2]:
        copy.wait()
    text_term[...] = dot(texts_ref[...], head_ref[...], 0, 0)
    copies[2].wait()
    pre_act = None
    for cut, copy in zip(cuts, copies[3 : 3 + CUTS]):
        copy.wait()
        part = dot(fc_in_ref[:, cut], images_ref[:, cut], 1, 1)
        pre_act = part if pre_act is None else pre_act + part
    square = pre_act * pre_act
    bent = jnp.tanh(GELU_SCALE * pre_act * (1.0 + GELU_CUBIC * square))
    activation = (0.5 * pre_act * (1.0 + bent)).astype(jnp.bfloat16)
    slope_ref[...] = 0.5 * (1.0 + bent) + (
        0.5 * GELU_SCALE * pre_act * (1.0 - bent * bent) * (1.0 + 3.0 * GELU_CUBIC * square)
    )
    for cut, copy in zip(cuts, copies[3 + CUTS :]):
        copy.wait()
        image_term[:, cut] = dot(activation, fc_out_ref[:, cut], 0, 0)
    for first, term in ((0, image_term), (HALF, text_term)):
        kept_ref[first : first + HALF] = own_half(term, core)
        sent_ref[first : first + HALF] = own_half(term, 1 - core).astype(jnp.bfloat16)


def unit_kernel(core_ref, chips_ref, images_ref, unit_ref, inverse_ref, sent_ref):
    embed = chips_ref[0].astype(jnp.float32) + chips_ref[1].astype(jnp.float32)
    image_embed = own_half(images_ref, core_ref[0]).astype(jnp.float32) + embed[:HALF]
    for first, rows in ((0, image_embed), (HALF, embed[HALF:])):
        inverse = lax.rsqrt(jnp.sum(rows * rows, axis=1, keepdims=True) + epsilon)
        unit = rows * inverse
        unit_ref[first : first + HALF] = unit
        inverse_ref[first : first + HALF] = jnp.broadcast_to(inverse, (HALF, LANES))
        sent_ref[first : first + HALF] = unit.astype(jnp.bfloat16)


def split_loss(loss):
    high = loss.astype(jnp.bfloat16).astype(jnp.float32)
    lanes = lax.broadcasted_iota(jnp.int32, (loss.shape[0], LANES), 1)
    return jnp.where(lanes == 0, high, jnp.where(lanes == 1, loss - high, 0.0))


def pair_terms(own, others, positive):
    logits = logit_scale * dot(own, others, 1, 1) + logit_bias
    if positive is None:
        flipped = logits
    else:
        flipped = jnp.where(positive, -logits, logits)
    small = jnp.exp(-jnp.abs(flipped))
    loss = jnp.maximum(flipped, 0.0) + jnp.log1p(small)
    sigmoid = jnp.where(flipped >= 0.0, 1.0, small) / (1.0 + small)
    if positive is None:
        pair_grad = loss_scale * sigmoid
    else:
        pair_grad = jnp.where(positive, -loss_scale, loss_scale) * sigmoid
    return logit_scale * dot(pair_grad.astype(jnp.bfloat16), others, 1, 0), loss


def score_kernel(
    core_ref, image_ref, text_ref, near_text_ref, far_text_ref, near_image_ref, far_image_ref,
    column_ref, row_ref, kept_ref, sent_ref, image_part, text_part,
):
    core = core_ref[0]
    rows, width = image_ref.shape
    across = lax.broadcasted_iota(jnp.int32, (rows, rows), 1)
    down = lax.broadcasted_iota(jnp.int32, (rows, rows), 0)
    near, near_loss = pair_terms(image_ref[...], near_text_ref[...], across == column_ref[...])
    far, far_loss = pair_terms(image_ref[...], far_text_ref[...], None)
    image_part[:, :width] = near + far
    image_part[:, width:] = split_loss(jnp.sum(near_loss + far_loss, axis=1, keepdims=True))
    near, unused = pair_terms(text_ref[...], near_image_ref[...], down == row_ref[...])
    far, unused = pair_terms(text_ref[...], far_image_ref[...], None)
    text_part[:, :width] = near + far
    text_part[:, width:] = jnp.zeros((rows, LANES), jnp.float32)
    for first, part in ((0, image_part), (HALF, text_part)):
        kept_ref[first : first + HALF] = own_half(part, core)
        sent_ref[first : first + HALF] = own_half(part, 1 - core).astype(jnp.bfloat16)


def tangent_kernel(chips_ref, unit_ref, inverse_ref, sent_ref):
    width = unit_ref.shape[1]
    sums = chips_ref[0].astype(jnp.float32) + chips_ref[1].astype(jnp.float32)
    grad, unit = sums[:, :width], unit_ref[...]
    along = jnp.sum(unit * grad, axis=1, keepdims=True)
    tangent = (grad - unit * along) * inverse_ref[:, :1]
    sent_ref[:, :width] = tangent.astype(jnp.bfloat16)
    loss = sums[:, width : width + 1] + sums[:, width + 1 : width + 2]
    sent_ref[:, width:] = split_loss(loss).astype(jnp.bfloat16)


def backward_kernel(
    grads_ref, slope_ref, fc_out_ref, head_ref, hidden_ref, text_ref, loss_ref
):
    rows, width = 2 * HALF, fc_out_ref.shape[1]
    image_grad = grads_ref[:, :HALF].reshape(rows, width + LANES)
    text_grad = grads_ref[:, HALF:].reshape(rows, width + LANES)
    losses = jnp.sum(image_grad[:, width:].astype(jnp.float32), axis=1, keepdims=True)
    loss_ref[...] = jnp.broadcast_to(losses, (rows, LANES)).T[:1] / (WINDOW * rows)
    act_grad = dot(fc_out_ref[...], image_grad[:, :width], 1, 1)
    hidden_ref[...] = (slope_ref[...] * act_grad).astype(jnp.bfloat16)
    text_ref[...] = dot(head_ref[...], text_grad[:, :width], 1, 1).astype(jnp.bfloat16)


def kernel(body, outs, scratch=(), places="", vmem=24):
    spaces = dict(s=pltpu.SMEM, v=pltpu.VMEM, h=pltpu.HBM)
    return pl.pallas_call(
        body,
        out_shape=[jax.ShapeDtypeStruct(shape, dtype) for shape, dtype in outs],
        in_specs=[pl.BlockSpec(memory_space=spaces[place]) for place in places],
        out_specs=[pl.BlockSpec(memory_space=pltpu.VMEM) for unused in outs],
        scratch_shapes=list(scratch),
        compiler_params=pltpu.CompilerParams(vmem_limit_bytes=vmem * 1024 * 1024),
    )


def chip_gather(kept, sent, core):
    got = lax.dynamic_index_in_dim(lax.all_gather(sent, "core"), 1 - core[0], 0, False)
    return lax.all_gather((kept + got.astype(jnp.float32)).astype(jnp.bfloat16), "y_hi")


def local(images, texts, fc_in, fc_out, head, partner):
    rows, width = images.shape
    hidden, features = fc_out.shape[0], head.shape[0]
    f32, bf16 = jnp.float32, jnp.bfloat16
    core = lax.axis_index("core")
    role = 2 * (lax.axis_index("y_hi") ^ (lax.axis_index("z") & 1)) + core
    core = core.reshape(1)

    slope, kept, sent = kernel(
        heads_kernel,
        [((hidden, rows), f32), ((rows, width), f32), ((rows, width), bf16)],
        [
            pltpu.VMEM((features, rows), bf16),
            pltpu.VMEM((features, width), bf16),
            pltpu.VMEM((rows, width), bf16),
            pltpu.VMEM((hidden, width), bf16),
            pltpu.VMEM((hidden, width), bf16),
            pltpu.VMEM((rows, width), f32),
            pltpu.VMEM((rows, width), f32),
            pltpu.SemaphoreType.DMA((3 + 2 * CUTS,)),
        ],
        "shhhhh",
        vmem=HEADS_VMEM,
    )(core, texts.T, head, images, fc_in.T, fc_out)

    unit, inverse, unit_sent = kernel(
        unit_kernel,
        [((rows, width), f32), ((rows, LANES), f32), ((rows, width), bf16)],
        places="svv",
    )(core, chip_gather(kept, sent, core), images)

    units = lax.all_gather(unit_sent, "core")
    image_own = units[:, :HALF].reshape(rows, width)
    text_own = units[:, HALF:].reshape(rows, width)
    near_text = move(text_own, lambda role: OFFSET[role])
    near_image = move(image_own, lambda role: -OFFSET[role])
    far_text = move(near_text, lambda role: NEAR)
    far_image = move(near_image, lambda role: -NEAR)

    paired = jnp.where(role == 0, partner, -1)
    columns = width + LANES
    kept, sent = kernel(
        score_kernel,
        [((rows, columns), f32), ((rows, columns), bf16)],
        [pltpu.VMEM((rows, columns), f32), pltpu.VMEM((rows, columns), f32)],
        "svvvvvvvv",
    )(
        core, image_own, text_own, near_text, far_text, near_image, far_image,
        paired.reshape(rows, 1), paired.reshape(1, rows),
    )

    (grads,) = kernel(tangent_kernel, [((rows, columns), bf16)], places="vvv")(
        chip_gather(kept, sent, core), unit, inverse
    )
    hidden_grad, text_grad, loss = kernel(
        backward_kernel,
        [((hidden, rows), bf16), ((features, rows), bf16), ((1, rows), f32)],
        places="vvvv",
    )(lax.all_gather(grads, "core"), slope, fc_out, head)
    return (hidden_grad.T, text_grad.T, loss.reshape(rows))


def solution(mesh):
    dp = ("z", "y_lo", "x")
    return jax.shard_map(
        local,
        mesh=Mesh(mesh.devices.reshape(SIZES), AXES),
        in_specs=(P(dp, None), P(dp, MP), P(None, MP), P(MP, None), P(MP, None), P(dp)),
        out_specs=(P(dp, MP), P(dp, MP), P(dp)),
        check_vma=False,
    )
```

```python
import jax
import jax.numpy as jnp
from jax import lax
from jax.experimental import pallas as pl
from jax.experimental.pallas import tpu as pltpu
from jax.sharding import Mesh, PartitionSpec as P

WINDOW = 8


logit_scale = 32.0
logit_bias = -2.0
loss_scale = 16.0
epsilon = 1e-06

AXES = ("z", "y_lo", "x", "y_hi", "core")
SIZES = (16, 4, 4, 2, 2)
MP = ("y_hi", "core")
NEAR = 4
OFFSET = (0, 2, 1, 3)
HALF = 64
LANES = 128
HEADS_VMEM = 56
CUTS = 3
GELU_SCALE = 0.7978845608028654
GELU_CUBIC = 0.044715


def place(block, role):
    z = block // 16
    y_hi = (role // 2) ^ (z & 1)
    return block * 4 + y_hi * 2 + role % 2


def moves(shift):
    return [
        (place(block, role), place((block + shift(role)) % 256, role))
        for block in range(256)
        for role in range(4)
    ]


def move(value, shift):
    return lax.ppermute(value, AXES, moves(shift))


def dot(left, right, left_dim, right_dim):
    return lax.dot_general(
        left, right, (((left_dim,), (right_dim,)), ((), ())), preferred_element_type=jnp.float32
    )


def own_half(array, core):
    return array[pl.ds(pl.multiple_of(core * HALF, HALF), HALF), :]


def heads_kernel(
    core_ref, texts_hbm, head_hbm, images_hbm, fc_in_hbm, fc_out_hbm,
    slope_ref, kept_ref, sent_ref,
    texts_ref, head_ref, images_ref, fc_in_ref, fc_out_ref, image_term, text_term, sems,
):
    core = core_ref[0]
    width = images_ref.shape[1]
    cuts = [pl.ds(first, width // CUTS) for first in range(0, width, width // CUTS)]
    pairs = [(texts_hbm, texts_ref), (head_hbm, head_ref), (images_hbm, images_ref)]
    for source, target in ((fc_in_hbm, fc_in_ref), (fc_out_hbm, fc_out_ref)):
        pairs += [(source.at[:, cut], target.at[:, cut]) for cut in cuts]
    copies = [
        pltpu.make_async_copy(source, target, sems.at[index])
        for index, (source, target) in enumerate(pairs)
    ]
    for copy in copies:
        copy.start()
    for copy in copies[:2]:
        copy.wait()
    text_term[...] = dot(texts_ref[...], head_ref[...], 0, 0)
    copies[2].wait()
    pre_act = None
    for cut, copy in zip(cuts, copies[3 : 3 + CUTS]):
        copy.wait()
        part = dot(fc_in_ref[:, cut], images_ref[:, cut], 1, 1)
        pre_act = part if pre_act is None else pre_act + part
    square = pre_act * pre_act
    bent = jnp.tanh(GELU_SCALE * pre_act * (1.0 + GELU_CUBIC * square))
    activation = (0.5 * pre_act * (1.0 + bent)).astype(jnp.bfloat16)
    slope_ref[...] = 0.5 * (1.0 + bent) + (
        0.5 * GELU_SCALE * pre_act * (1.0 - bent * bent) * (1.0 + 3.0 * GELU_CUBIC * square)
    )
    for cut, copy in zip(cuts, copies[3 + CUTS :]):
        copy.wait()
        image_term[:, cut] = dot(activation, fc_out_ref[:, cut], 0, 0)
    for first, term in ((0, image_term), (HALF, text_term)):
        kept_ref[first : first + HALF] = own_half(term, core)
        sent_ref[first : first + HALF] = own_half(term, 1 - core).astype(jnp.bfloat16)


def unit_kernel(
    core_ref, chips_ref, images_ref, unit_ref, inverse_ref, image_sent_ref, text_sent_ref
):
    embed = chips_ref[0].astype(jnp.float32) + chips_ref[1].astype(jnp.float32)
    image_embed = own_half(images_ref, core_ref[0]).astype(jnp.float32) + embed[:HALF]
    for first, rows in ((0, image_embed), (HALF, embed[HALF:])):
        inverse = lax.rsqrt(jnp.sum(rows * rows, axis=1, keepdims=True) + epsilon)
        unit = rows * inverse
        unit_ref[first : first + HALF] = unit
        inverse_ref[first : first + HALF] = jnp.broadcast_to(inverse, (HALF, LANES))
        sent = text_sent_ref if first else image_sent_ref
        sent[...] = unit.astype(jnp.bfloat16)


def split_loss(loss):
    high = loss.astype(jnp.bfloat16).astype(jnp.float32)
    lanes = lax.broadcasted_iota(jnp.int32, (loss.shape[0], LANES), 1)
    return jnp.where(lanes == 0, high, jnp.where(lanes == 1, loss - high, 0.0))


def pair_terms(own, others, positive):
    logits = logit_scale * dot(own, others, 1, 1) + logit_bias
    if positive is None:
        flipped = logits
    else:
        flipped = jnp.where(positive, -logits, logits)
    small = jnp.exp(-jnp.abs(flipped))
    loss = jnp.maximum(flipped, 0.0) + jnp.log1p(small)
    sigmoid = jnp.where(flipped >= 0.0, 1.0, small) / (1.0 + small)
    if positive is None:
        pair_grad = loss_scale * sigmoid
    else:
        pair_grad = jnp.where(positive, -loss_scale, loss_scale) * sigmoid
    return logit_scale * dot(pair_grad.astype(jnp.bfloat16), others, 1, 0), loss


def image_kernel(
    core_ref, own_ref, near_ref, far_ref, column_ref, kept_ref, sent_ref, part_ref
):
    core = core_ref[0]
    rows, width = own_ref.shape
    across = lax.broadcasted_iota(jnp.int32, (rows, rows), 1)
    near, near_loss = pair_terms(own_ref[...], near_ref[...], across == column_ref[...])
    far, far_loss = pair_terms(own_ref[...], far_ref[...], None)
    part_ref[:, :width] = near + far
    part_ref[:, width:] = split_loss(jnp.sum(near_loss + far_loss, axis=1, keepdims=True))
    kept_ref[...] = own_half(part_ref, core)
    sent_ref[...] = own_half(part_ref, 1 - core).astype(jnp.bfloat16)


def text_kernel(
    core_ref, own_ref, near_ref, far_ref, row_ref, image_kept_ref, image_sent_ref,
    kept_ref, sent_ref, part_ref,
):
    core = core_ref[0]
    rows, width = own_ref.shape
    down = lax.broadcasted_iota(jnp.int32, (rows, rows), 0)
    near, unused = pair_terms(own_ref[...], near_ref[...], down == row_ref[...])
    far, unused = pair_terms(own_ref[...], far_ref[...], None)
    part_ref[:, :width] = near + far
    part_ref[:, width:] = jnp.zeros((rows, LANES), jnp.float32)
    kept_ref[:HALF] = image_kept_ref[...]
    sent_ref[:HALF] = image_sent_ref[...]
    kept_ref[HALF:] = own_half(part_ref, core)
    sent_ref[HALF:] = own_half(part_ref, 1 - core).astype(jnp.bfloat16)


def tangent_kernel(chips_ref, unit_ref, inverse_ref, sent_ref):
    width = unit_ref.shape[1]
    sums = chips_ref[0].astype(jnp.float32) + chips_ref[1].astype(jnp.float32)
    grad, unit = sums[:, :width], unit_ref[...]
    along = jnp.sum(unit * grad, axis=1, keepdims=True)
    tangent = (grad - unit * along) * inverse_ref[:, :1]
    sent_ref[:, :width] = tangent.astype(jnp.bfloat16)
    loss = sums[:, width : width + 1] + sums[:, width + 1 : width + 2]
    sent_ref[:, width:] = split_loss(loss).astype(jnp.bfloat16)


def backward_kernel(
    grads_ref, slope_ref, fc_out_ref, head_ref, hidden_ref, text_ref, loss_ref
):
    rows, width = 2 * HALF, fc_out_ref.shape[1]
    image_grad = grads_ref[:, :HALF].reshape(rows, width + LANES)
    text_grad = grads_ref[:, HALF:].reshape(rows, width + LANES)
    losses = jnp.sum(image_grad[:, width:].astype(jnp.float32), axis=1, keepdims=True)
    loss_ref[...] = jnp.broadcast_to(losses, (rows, LANES)).T[:1] / (WINDOW * rows)
    act_grad = dot(fc_out_ref[...], image_grad[:, :width], 1, 1)
    hidden_ref[...] = (slope_ref[...] * act_grad).astype(jnp.bfloat16)
    text_ref[...] = dot(head_ref[...], text_grad[:, :width], 1, 1).astype(jnp.bfloat16)


def kernel(body, outs, scratch=(), places="", vmem=24):
    spaces = dict(s=pltpu.SMEM, v=pltpu.VMEM, h=pltpu.HBM)
    return pl.pallas_call(
        body,
        out_shape=[jax.ShapeDtypeStruct(shape, dtype) for shape, dtype in outs],
        in_specs=[pl.BlockSpec(memory_space=spaces[place]) for place in places],
        out_specs=[pl.BlockSpec(memory_space=pltpu.VMEM) for unused in outs],
        scratch_shapes=list(scratch),
        compiler_params=pltpu.CompilerParams(vmem_limit_bytes=vmem * 1024 * 1024),
    )


def chip_gather(kept, sent, core):
    got = lax.dynamic_index_in_dim(lax.all_gather(sent, "core"), 1 - core[0], 0, False)
    return lax.all_gather((kept + got.astype(jnp.float32)).astype(jnp.bfloat16), "y_hi")


def local(images, texts, fc_in, fc_out, head, partner):
    rows, width = images.shape
    hidden, features = fc_out.shape[0], head.shape[0]
    f32, bf16 = jnp.float32, jnp.bfloat16
    core = lax.axis_index("core")
    role = 2 * (lax.axis_index("y_hi") ^ (lax.axis_index("z") & 1)) + core
    core = core.reshape(1)

    slope, kept, sent = kernel(
        heads_kernel,
        [((hidden, rows), f32), ((rows, width), f32), ((rows, width), bf16)],
        [
            pltpu.VMEM((features, rows), bf16),
            pltpu.VMEM((features, width), bf16),
            pltpu.VMEM((rows, width), bf16),
            pltpu.VMEM((hidden, width), bf16),
            pltpu.VMEM((hidden, width), bf16),
            pltpu.VMEM((rows, width), f32),
            pltpu.VMEM((rows, width), f32),
            pltpu.SemaphoreType.DMA((3 + 2 * CUTS,)),
        ],
        "shhhhh",
        vmem=HEADS_VMEM,
    )(core, texts.T, head, images, fc_in.T, fc_out)

    unit, inverse, *unit_sent = kernel(
        unit_kernel,
        [((rows, width), f32), ((rows, LANES), f32)] + [((HALF, width), bf16)] * 2,
        places="svv",
    )(core, chip_gather(kept, sent, core), images)

    text_own = lax.all_gather(unit_sent[1], "core", tiled=True)
    text_own, image_sent = lax.optimization_barrier((text_own, unit_sent[0]))
    near_text = move(text_own, lambda role: OFFSET[role])
    image_own = lax.all_gather(image_sent, "core", tiled=True)
    near_image = move(image_own, lambda role: -OFFSET[role])
    far_text = move(near_text, lambda role: NEAR)
    far_image = move(near_image, lambda role: -NEAR)

    paired = jnp.where(role == 0, partner, -1)
    columns = width + LANES
    part = [pltpu.VMEM((rows, columns), f32)]
    image_parts = kernel(
        image_kernel, [((HALF, columns), f32), ((HALF, columns), bf16)], part, "svvvv"
    )(core, image_own, near_text, far_text, paired.reshape(rows, 1))
    kept, sent = kernel(
        text_kernel, [((rows, columns), f32), ((rows, columns), bf16)], part, "svvvvvv"
    )(core, text_own, near_image, far_image, paired.reshape(1, rows), *image_parts)

    (grads,) = kernel(tangent_kernel, [((rows, columns), bf16)], places="vvv")(
        chip_gather(kept, sent, core), unit, inverse
    )
    hidden_grad, text_grad, loss = kernel(
        backward_kernel,
        [((hidden, rows), bf16), ((features, rows), bf16), ((1, rows), f32)],
        places="vvvv",
    )(lax.all_gather(grads, "core"), slope, fc_out, head)
    return (hidden_grad.T, text_grad.T, loss.reshape(rows))


def solution(mesh):
    dp = ("z", "y_lo", "x")
    return jax.shard_map(
        local,
        mesh=Mesh(mesh.devices.reshape(SIZES), AXES),
        in_specs=(P(dp, None), P(dp, MP), P(None, MP), P(MP, None), P(MP, None), P(dp)),
        out_specs=(P(dp, MP), P(dp, MP), P(dp)),
        check_vma=False,
    )
```

```python
import jax
import jax.numpy as jnp
from jax import lax
from jax.experimental import pallas as pl
from jax.experimental.pallas import tpu as pltpu
from jax.sharding import Mesh, PartitionSpec as P

WINDOW = 8


logit_scale = 32.0
logit_bias = -2.0
loss_scale = 16.0
epsilon = 1e-06

AXES = ("z", "y_lo", "x", "y_hi", "core")
SIZES = (16, 4, 4, 2, 2)
MP = ("y_hi", "core")
FIRST = (1, 2)
SECOND = (4, 3)
RELAY = 4
HALF = 64
LANES = 128
HEADS_VMEM = 56
CUTS = 3
GELU_SCALE = 0.7978845608028654
GELU_CUBIC = 0.044715


def place(block, role):
    z = block // 16
    y_hi = (role // 2) ^ (z & 1)
    return block * 4 + y_hi * 2 + role % 2


def move(value, steps):
    pairs = [
        (place(block, role), place((block + (1 - role // 2 * 2) * steps[role % 2]) % 256, role))
        for block in range(256)
        for role in range(4)
        if steps[role % 2]
    ]
    return lax.ppermute(value, AXES, pairs)


def dot(left, right, left_dim, right_dim):
    return lax.dot_general(
        left, right, (((left_dim,), (right_dim,)), ((), ())), preferred_element_type=jnp.float32
    )


def own_half(array, core):
    return array[pl.ds(pl.multiple_of(core * HALF, HALF), HALF), :]


def heads_kernel(
    place_ref, texts_hbm, head_hbm, images_hbm, fc_in_hbm, fc_out_hbm,
    slope_ref, kept_ref, sent_ref,
    texts_ref, head_ref, images_ref, fc_in_ref, fc_out_ref, image_term, text_term, sems,
):
    core = place_ref[0]
    width = images_ref.shape[1]
    cuts = [pl.ds(first, width // CUTS) for first in range(0, width, width // CUTS)]
    pairs = [(texts_hbm, texts_ref), (head_hbm, head_ref), (images_hbm, images_ref)]
    for source, target in ((fc_in_hbm, fc_in_ref), (fc_out_hbm, fc_out_ref)):
        pairs += [(source.at[:, cut], target.at[:, cut]) for cut in cuts]
    copies = [
        pltpu.make_async_copy(source, target, sems.at[index])
        for index, (source, target) in enumerate(pairs)
    ]
    for copy in copies:
        copy.start()
    for copy in copies[:2]:
        copy.wait()
    text_term[...] = dot(texts_ref[...], head_ref[...], 0, 0)
    copies[2].wait()
    pre_act = None
    for cut, copy in zip(cuts, copies[3 : 3 + CUTS]):
        copy.wait()
        part = dot(fc_in_ref[:, cut], images_ref[:, cut], 1, 1)
        pre_act = part if pre_act is None else pre_act + part
    square = pre_act * pre_act
    bent = jnp.tanh(GELU_SCALE * pre_act * (1.0 + GELU_CUBIC * square))
    activation = (0.5 * pre_act * (1.0 + bent)).astype(jnp.bfloat16)
    slope_ref[...] = 0.5 * (1.0 + bent) + (
        0.5 * GELU_SCALE * pre_act * (1.0 - bent * bent) * (1.0 + 3.0 * GELU_CUBIC * square)
    )
    for cut, copy in zip(cuts, copies[3 + CUTS :]):
        copy.wait()
        image_term[:, cut] = dot(activation, fc_out_ref[:, cut], 0, 0)
    for first, term in ((0, image_term), (HALF, text_term)):
        kept_ref[first : first + HALF] = own_half(term, core)
        sent_ref[first : first + HALF] = own_half(term, 1 - core).astype(jnp.bfloat16)


def unit_kernel(
    place_ref, chips_ref, images_ref, unit_ref, inverse_ref, own_sent_ref, moved_sent_ref
):
    embed = chips_ref[0].astype(jnp.float32) + chips_ref[1].astype(jnp.float32)
    image_embed = own_half(images_ref, place_ref[0]).astype(jnp.float32) + embed[:HALF]
    units = []
    for first, rows in ((0, image_embed), (HALF, embed[HALF:])):
        inverse = lax.rsqrt(jnp.sum(rows * rows, axis=1, keepdims=True) + epsilon)
        units.append(rows * inverse)
        unit_ref[first : first + HALF] = units[-1]
        inverse_ref[first : first + HALF] = jnp.broadcast_to(inverse, (HALF, LANES))
    image_side = place_ref[1] == 0
    own_sent_ref[...] = jnp.where(image_side, units[0], units[1]).astype(jnp.bfloat16)
    moved_sent_ref[...] = jnp.where(image_side, units[1], units[0]).astype(jnp.bfloat16)


def split_loss(loss):
    high = loss.astype(jnp.bfloat16).astype(jnp.float32)
    lanes = lax.broadcasted_iota(jnp.int32, (loss.shape[0], LANES), 1)
    return jnp.where(lanes == 0, high, jnp.where(lanes == 1, loss - high, 0.0))


def pair_terms(own, others, positive):
    logits = logit_scale * dot(own, others, 1, 1) + logit_bias
    if positive is None:
        flipped = logits
    else:
        flipped = jnp.where(positive, -logits, logits)
    small = jnp.exp(-jnp.abs(flipped))
    loss = jnp.maximum(flipped, 0.0) + jnp.log1p(small)
    sigmoid = jnp.where(flipped >= 0.0, 1.0, small) / (1.0 + small)
    if positive is None:
        pair_grad = loss_scale * sigmoid
    else:
        pair_grad = jnp.where(positive, -loss_scale, loss_scale) * sigmoid
    return logit_scale * dot(pair_grad.astype(jnp.bfloat16), others, 1, 0), loss


def early_kernel(own_ref, first_ref, second_ref, part_ref):
    rows, width = own_ref.shape
    own = own_ref[...]
    first, first_loss = pair_terms(own, first_ref[...], None)
    second, second_loss = pair_terms(own, second_ref[...], None)
    part_ref[:, :width] = first + second
    loss = jnp.sum(first_loss + second_loss, axis=1, keepdims=True)
    part_ref[:, width:] = jnp.broadcast_to(loss, (rows, LANES))


def late_kernel(
    place_ref, own_ref, here_ref, third_ref, fourth_ref, column_ref, row_ref, early_ref,
    kept_ref, sent_ref, part_ref,
):
    core = place_ref[0]
    rows, width = own_ref.shape
    own = own_ref[...]
    across = lax.broadcasted_iota(jnp.int32, (rows, rows), 1) == column_ref[...]
    down = lax.broadcasted_iota(jnp.int32, (rows, rows), 0) == row_ref[...]
    paired = jnp.where(place_ref[1] == 0, across.astype(jnp.int32), down.astype(jnp.int32))
    third, third_loss = pair_terms(own, third_ref[...], None)
    last = jnp.where(core == 0, here_ref[...], fourth_ref[...])
    last, last_loss = pair_terms(own, last, paired == 1)
    part_ref[:, :width] = early_ref[:, :width] + third + last
    loss = jnp.sum(third_loss + last_loss, axis=1, keepdims=True)
    part_ref[:, width:] = split_loss(early_ref[:, width : width + 1] + loss)
    kept_ref[...] = own_half(part_ref, core)
    sent_ref[...] = own_half(part_ref, 1 - core).astype(jnp.bfloat16)


def tangent_kernel(place_ref, kept_ref, swapped_ref, unit_ref, inverse_ref, sent_ref):
    width = unit_ref.shape[1]
    sums = kept_ref[...] + swapped_ref[1 - place_ref[0]].astype(jnp.float32)
    side = pl.ds(pl.multiple_of(place_ref[1] * HALF, HALF), HALF)
    grad, unit = sums[:, :width], unit_ref[side, :]
    along = jnp.sum(unit * grad, axis=1, keepdims=True)
    tangent = (grad - unit * along) * inverse_ref[side, :][:, :1]
    sent_ref[:, :width] = tangent.astype(jnp.bfloat16)
    loss = sums[:, width : width + 1] + sums[:, width + 1 : width + 2]
    sent_ref[:, width:] = split_loss(loss).astype(jnp.bfloat16)


def backward_kernel(
    place_ref, grads_ref, slope_ref, fc_out_ref, head_ref, hidden_ref, text_ref, loss_ref
):
    rows, width = 2 * HALF, fc_out_ref.shape[1]
    image_chip = place_ref[2] * 2
    image_grad = grads_ref[pl.ds(image_chip, 2)].reshape(rows, width + LANES)
    text_grad = grads_ref[pl.ds(2 - image_chip, 2)].reshape(rows, width + LANES)
    losses = jnp.sum(image_grad[:, width:].astype(jnp.float32), axis=1, keepdims=True)
    loss_ref[...] = jnp.broadcast_to(losses, (rows, LANES)).T[:1] / (WINDOW * rows)
    act_grad = dot(fc_out_ref[...], image_grad[:, :width], 1, 1)
    hidden_ref[...] = (slope_ref[...] * act_grad).astype(jnp.bfloat16)
    text_ref[...] = dot(head_ref[...], text_grad[:, :width], 1, 1).astype(jnp.bfloat16)


def kernel(body, outs, scratch=(), places="", vmem=24):
    spaces = dict(s=pltpu.SMEM, v=pltpu.VMEM, h=pltpu.HBM)
    return pl.pallas_call(
        body,
        out_shape=[jax.ShapeDtypeStruct(shape, dtype) for shape, dtype in outs],
        in_specs=[pl.BlockSpec(memory_space=spaces[place]) for place in places],
        out_specs=[pl.BlockSpec(memory_space=pltpu.VMEM) for unused in outs],
        scratch_shapes=list(scratch),
        compiler_params=pltpu.CompilerParams(vmem_limit_bytes=vmem * 1024 * 1024),
    )


def local(images, texts, fc_in, fc_out, head, partner):
    rows, width = images.shape
    hidden, features = fc_out.shape[0], head.shape[0]
    f32, bf16 = jnp.float32, jnp.bfloat16
    core, flip = lax.axis_index("core"), lax.axis_index("z") & 1
    here = jnp.stack([core, lax.axis_index("y_hi") ^ flip, flip])

    slope, kept, sent = kernel(
        heads_kernel,
        [((hidden, rows), f32), ((rows, width), f32), ((rows, width), bf16)],
        [
            pltpu.VMEM((features, rows), bf16),
            pltpu.VMEM((features, width), bf16),
            pltpu.VMEM((rows, width), bf16),
            pltpu.VMEM((hidden, width), bf16),
            pltpu.VMEM((hidden, width), bf16),
            pltpu.VMEM((rows, width), f32),
            pltpu.VMEM((rows, width), f32),
            pltpu.SemaphoreType.DMA((3 + 2 * CUTS,)),
        ],
        "shhhhh",
        vmem=HEADS_VMEM,
    )(here, texts.T, head, images, fc_in.T, fc_out)
    got = lax.dynamic_index_in_dim(lax.all_gather(sent, "core"), 1 - core, 0, False)
    chips = lax.all_gather((kept + got.astype(f32)).astype(bf16), "y_hi")

    unit, inverse, own_sent, moved_sent = kernel(
        unit_kernel,
        [((rows, width), f32), ((rows, LANES), f32)] + [((HALF, width), bf16)] * 2,
        places="svv",
    )(here, chips, images)

    moved = lax.all_gather(moved_sent, "core", tiled=True)
    moved, own_sent = lax.optimization_barrier((moved, own_sent))
    first = move(moved, FIRST)
    second = move(moved, SECOND)
    own = lax.all_gather(own_sent, "core", tiled=True)
    third = move(first, (RELAY, RELAY))
    fourth = move(second, (0, RELAY))

    paired = jnp.where(core == 0, partner, -1)
    columns = width + LANES
    part = [((rows, columns), f32)]
    (early,) = kernel(early_kernel, part, places="vvv")(own, first, second)
    kept, sent = kernel(
        late_kernel,
        [((HALF, columns), f32), ((HALF, columns), bf16)],
        [pltpu.VMEM(*part[0])],
        "svvvvvvv",
    )(here, own, moved, third, fourth, paired.reshape(rows, 1), paired.reshape(1, rows), early)

    (grads,) = kernel(tangent_kernel, [((HALF, columns), bf16)], places="svvvv")(
        here, kept, lax.all_gather(sent, "core"), unit, inverse
    )
    hidden_grad, text_grad, loss = kernel(
        backward_kernel,
        [((hidden, rows), bf16), ((features, rows), bf16), ((1, rows), f32)],
        places="svvvv",
    )(here, lax.all_gather(grads, MP), slope, fc_out, head)
    return (hidden_grad.T, text_grad.T, loss.reshape(rows))


def solution(mesh):
    dp = ("z", "y_lo", "x")
    return jax.shard_map(
        local,
        mesh=Mesh(mesh.devices.reshape(SIZES), AXES),
        in_specs=(P(dp, None), P(dp, MP), P(None, MP), P(MP, None), P(MP, None), P(dp)),
        out_specs=(P(dp, MP), P(dp, MP), P(dp)),
        check_vma=False,
    )
```

```python
import jax
import jax.numpy as jnp
from jax import lax
from jax.experimental import pallas as pl
from jax.experimental.pallas import tpu as pltpu
from jax.sharding import Mesh, PartitionSpec as P

WINDOW = 8


logit_scale = 32.0
logit_bias = -2.0
loss_scale = 16.0
epsilon = 1e-06

AXES = ("z", "y_lo", "x", "y_hi", "core")
SIZES = (16, 4, 4, 2, 2)
MP = ("y_hi", "core")
FIRST = (1, 3)
SECOND = (4, 2)
RELAY = 4
HALF = 64
LANES = 128
HEADS_VMEM = 56
CUTS = 3
GELU_SCALE = 0.7978845608028654
GELU_CUBIC = 0.044715


def place(block, role):
    z = block // 16
    y_hi = (role // 2) ^ (z & 1)
    return block * 4 + y_hi * 2 + role % 2


def move(value, steps):
    pairs = [
        (place(block, role), place((block + (1 - role // 2 * 2) * steps[role % 2]) % 256, role))
        for block in range(256)
        for role in range(4)
        if steps[role % 2]
    ]
    return lax.ppermute(value, AXES, pairs)


def dot(left, right, left_dim, right_dim):
    return lax.dot_general(
        left, right, (((left_dim,), (right_dim,)), ((), ())), preferred_element_type=jnp.float32
    )


def here():
    flip = lax.axis_index("z") & 1
    return lax.axis_index("core"), lax.axis_index("y_hi") ^ flip, flip


def own_half(array, core):
    return array[pl.ds(pl.multiple_of(core * HALF, HALF), HALF), :]


def heads_kernel(
    texts_hbm, head_hbm, images_hbm, fc_in_hbm, fc_out_hbm,
    slope_hbm, kept_ref, sent_ref,
    slope_ref, texts_ref, head_ref, images_ref, fc_in_ref, fc_out_ref, image_term, text_term, sems,
):
    core, unused, unused = here()
    width = images_ref.shape[1]
    cuts = [pl.ds(first, width // CUTS) for first in range(0, width, width // CUTS)]
    pairs = [(texts_hbm, texts_ref), (head_hbm, head_ref), (images_hbm, images_ref)]
    for source, target in ((fc_in_hbm, fc_in_ref), (fc_out_hbm, fc_out_ref)):
        pairs += [(source.at[:, cut], target.at[:, cut]) for cut in cuts]
    copies = [
        pltpu.make_async_copy(source, target, sems.at[index])
        for index, (source, target) in enumerate(pairs)
    ]
    for copy in copies:
        copy.start()
    for copy in copies[:2]:
        copy.wait()
    text_term[...] = dot(texts_ref[...], head_ref[...], 0, 0)
    copies[2].wait()
    pre_act = None
    for cut, copy in zip(cuts, copies[3 : 3 + CUTS]):
        copy.wait()
        part = dot(fc_in_ref[:, cut], images_ref[:, cut], 1, 1)
        pre_act = part if pre_act is None else pre_act + part
    square = pre_act * pre_act
    bent = jnp.tanh(GELU_SCALE * pre_act * (1.0 + GELU_CUBIC * square))
    activation = (0.5 * pre_act * (1.0 + bent)).astype(jnp.bfloat16)
    slope_ref[...] = 0.5 * (1.0 + bent) + (
        0.5 * GELU_SCALE * pre_act * (1.0 - bent * bent) * (1.0 + 3.0 * GELU_CUBIC * square)
    )
    slope_copy = pltpu.make_async_copy(slope_ref, slope_hbm, sems.at[len(copies)])
    slope_copy.start()
    for cut, copy in zip(cuts, copies[3 + CUTS :]):
        copy.wait()
        image_term[:, cut] = dot(activation, fc_out_ref[:, cut], 0, 0)
    for first, term in ((0, image_term), (HALF, text_term)):
        kept_ref[first : first + HALF] = own_half(term, core).astype(jnp.bfloat16)
        sent_ref[first : first + HALF] = own_half(term, 1 - core).astype(jnp.bfloat16)
    slope_copy.wait()


def core_sum_kernel(kept_ref, swapped_ref, sum_ref):
    core, unused, unused = here()
    got = swapped_ref[1 - core].astype(jnp.float32)
    sum_ref[...] = (kept_ref[...].astype(jnp.float32) + got).astype(jnp.bfloat16)


def unit_kernel(
    chips_ref, images_ref, unit_ref, inverse_ref, own_sent_ref, moved_sent_ref
):
    core, side, unused = here()
    embed = chips_ref[0].astype(jnp.float32) + chips_ref[1].astype(jnp.float32)
    image_embed = own_half(images_ref, core).astype(jnp.float32) + embed[:HALF]
    units = []
    for first, rows in ((0, image_embed), (HALF, embed[HALF:])):
        inverse = lax.rsqrt(jnp.sum(rows * rows, axis=1, keepdims=True) + epsilon)
        units.append(rows * inverse)
        unit_ref[first : first + HALF] = units[-1]
        inverse_ref[first : first + HALF] = jnp.broadcast_to(inverse, (HALF, LANES))
    own_sent_ref[...] = jnp.where(side == 0, units[0], units[1]).astype(jnp.bfloat16)
    moved_sent_ref[...] = jnp.where(side == 0, units[1], units[0]).astype(jnp.bfloat16)


def split_loss(loss):
    high = loss.astype(jnp.bfloat16).astype(jnp.float32)
    lanes = lax.broadcasted_iota(jnp.int32, (loss.shape[0], LANES), 1)
    return jnp.where(lanes == 0, high, jnp.where(lanes == 1, loss - high, 0.0))


def pair_terms(own, others, positive):
    logits = logit_scale * dot(own, others, 1, 1) + logit_bias
    if positive is None:
        flipped = logits
    else:
        flipped = jnp.where(positive, -logits, logits)
    small = jnp.exp(-jnp.abs(flipped))
    loss = jnp.maximum(flipped, 0.0) + jnp.log1p(small)
    sigmoid = jnp.where(flipped >= 0.0, 1.0, small) / (1.0 + small)
    if positive is None:
        pair_grad = loss_scale * sigmoid
    else:
        pair_grad = jnp.where(positive, -loss_scale, loss_scale) * sigmoid
    return logit_scale * dot(pair_grad.astype(jnp.bfloat16), others, 1, 0), loss


def early_kernel(own_ref, first_ref, second_ref, part_ref):
    rows, width = own_ref.shape
    own = own_ref[...]
    first, first_loss = pair_terms(own, first_ref[...], None)
    second, second_loss = pair_terms(own, second_ref[...], None)
    part_ref[:, :width] = first + second
    loss = jnp.sum(first_loss + second_loss, axis=1, keepdims=True)
    part_ref[:, width:] = jnp.broadcast_to(loss, (rows, LANES))


def late_kernel(
    own_ref, moved_ref, third_ref, fourth_ref, column_ref, row_ref, early_ref,
    kept_ref, sent_ref, part_ref,
):
    core, side, unused = here()
    rows, width = own_ref.shape
    own = own_ref[...]
    across = lax.broadcasted_iota(jnp.int32, (rows, rows), 1) == column_ref[...]
    down = lax.broadcasted_iota(jnp.int32, (rows, rows), 0) == row_ref[...]
    paired = jnp.where(side == 0, across.astype(jnp.int32), down.astype(jnp.int32))
    third, third_loss = pair_terms(own, third_ref[...], None)
    last = jnp.where(core == 0, moved_ref[...], fourth_ref[...])
    last, last_loss = pair_terms(own, last, paired == 1)
    part_ref[:, :width] = early_ref[:, :width] + third + last
    loss = jnp.sum(third_loss + last_loss, axis=1, keepdims=True)
    part_ref[:, width:] = split_loss(early_ref[:, width : width + 1] + loss)
    kept_ref[...] = own_half(part_ref, core)
    sent_ref[...] = own_half(part_ref, 1 - core).astype(jnp.bfloat16)


def tangent_kernel(kept_ref, swapped_ref, unit_ref, inverse_ref, sent_ref):
    width = unit_ref.shape[1]
    core, side, unused = here()
    sums = kept_ref[...] + swapped_ref[1 - core].astype(jnp.float32)
    side = pl.ds(pl.multiple_of(side * HALF, HALF), HALF)
    grad, unit = sums[:, :width], unit_ref[side, :]
    along = jnp.sum(unit * grad, axis=1, keepdims=True)
    tangent = (grad - unit * along) * inverse_ref[side, :][:, :1]
    sent_ref[:, :width] = tangent.astype(jnp.bfloat16)
    loss = sums[:, width : width + 1] + sums[:, width + 1 : width + 2]
    sent_ref[:, width:] = split_loss(loss).astype(jnp.bfloat16)


def backward_kernel(
    grads_ref, slope_ref, fc_out_ref, head_ref, hidden_ref, text_ref, loss_ref
):
    rows, width = 2 * HALF, fc_out_ref.shape[1]
    unused, unused, flip = here()
    image_chip = flip * 2
    image_grad = grads_ref[pl.ds(image_chip, 2)].reshape(rows, width + LANES)
    text_grad = grads_ref[pl.ds(2 - image_chip, 2)].reshape(rows, width + LANES)
    losses = jnp.sum(image_grad[:, width:].astype(jnp.float32), axis=1, keepdims=True)
    loss_ref[...] = jnp.broadcast_to(losses, (rows, LANES)).T[:1] / (WINDOW * rows)
    act_grad = dot(fc_out_ref[...], image_grad[:, :width], 1, 1)
    hidden_ref[...] = (slope_ref[...] * act_grad).astype(jnp.bfloat16)
    text_ref[...] = dot(head_ref[...], text_grad[:, :width], 1, 1).astype(jnp.bfloat16)


def kernel(body, outs, scratch=(), places="", vmem=24, out_places=None):
    spaces = dict(v=pltpu.VMEM, h=pltpu.HBM)
    return pl.pallas_call(
        body,
        out_shape=[jax.ShapeDtypeStruct(shape, dtype) for shape, dtype in outs],
        in_specs=[pl.BlockSpec(memory_space=spaces[place]) for place in places],
        out_specs=[
            pl.BlockSpec(memory_space=spaces[place]) for place in out_places or "v" * len(outs)
        ],
        scratch_shapes=list(scratch),
        compiler_params=pltpu.CompilerParams(vmem_limit_bytes=vmem * 1024 * 1024),
    )


def local(images, texts, fc_in, fc_out, head, partner):
    rows, width = images.shape
    hidden, features = fc_out.shape[0], head.shape[0]
    f32, bf16 = jnp.float32, jnp.bfloat16
    slope, kept, sent = kernel(
        heads_kernel,
        [((hidden, rows), f32), ((rows, width), bf16), ((rows, width), bf16)],
        [
            pltpu.VMEM((hidden, rows), f32),
            pltpu.VMEM((features, rows), bf16),
            pltpu.VMEM((features, width), bf16),
            pltpu.VMEM((rows, width), bf16),
            pltpu.VMEM((hidden, width), bf16),
            pltpu.VMEM((hidden, width), bf16),
            pltpu.VMEM((rows, width), f32),
            pltpu.VMEM((rows, width), f32),
            pltpu.SemaphoreType.DMA((4 + 2 * CUTS,)),
        ],
        "hhhhh",
        vmem=HEADS_VMEM,
        out_places="hvv",
    )(texts.T, head, images, fc_in.T, fc_out)
    (core_sum,) = kernel(core_sum_kernel, [((rows, width), bf16)], places="vv")(
        kept, lax.all_gather(sent, "core")
    )
    chips = lax.all_gather(core_sum, "y_hi")

    unit, inverse, own_sent, moved_sent = kernel(
        unit_kernel,
        [((rows, width), f32), ((rows, LANES), f32)] + [((HALF, width), bf16)] * 2,
        places="vv",
    )(chips, images)

    moved = lax.all_gather(moved_sent, "core", tiled=True)
    moved, own_sent = lax.optimization_barrier((moved, own_sent))
    first = move(moved, FIRST)
    second = move(moved, SECOND)
    own = lax.all_gather(own_sent, "core", tiled=True)
    third = move(first, (RELAY, RELAY))
    fourth = move(second, (0, RELAY))

    paired = jnp.where(lax.axis_index("core") == 0, partner, -1)
    columns = width + LANES
    part = [((rows, columns), f32)]
    (early,) = kernel(early_kernel, part, places="vvv")(own, first, second)
    kept, sent = kernel(
        late_kernel,
        [((HALF, columns), f32), ((HALF, columns), bf16)],
        [pltpu.VMEM(*part[0])],
        "vvvvvvv",
    )(own, moved, third, fourth, paired.reshape(rows, 1), paired.reshape(1, rows), early)

    (grads,) = kernel(tangent_kernel, [((HALF, columns), bf16)], places="vvvv")(
        kept, lax.all_gather(sent, "core"), unit, inverse
    )
    hidden_grad, text_grad, loss = kernel(
        backward_kernel,
        [((hidden, rows), bf16), ((features, rows), bf16), ((1, rows), f32)],
        places="vvvv",
    )(lax.all_gather(grads, MP), slope, fc_out, head)
    return (hidden_grad.T, text_grad.T, loss.reshape(rows))


def solution(mesh):
    dp = ("z", "y_lo", "x")
    return jax.shard_map(
        local,
        mesh=Mesh(mesh.devices.reshape(SIZES), AXES),
        in_specs=(P(dp, None), P(dp, MP), P(None, MP), P(MP, None), P(MP, None), P(dp)),
        out_specs=(P(dp, MP), P(dp, MP), P(dp)),
        check_vma=False,
    )
```

```python
import jax
import jax.numpy as jnp
from jax import lax
from jax.experimental import pallas as pl
from jax.experimental.pallas import tpu as pltpu
from jax.sharding import Mesh, PartitionSpec as P

WINDOW = 8


logit_scale = 32.0
logit_bias = -2.0
loss_scale = 16.0
epsilon = 1e-06

AXES = ("z", "y_lo", "x", "y_hi", "core")
SIZES = (16, 4, 4, 2, 2)
MP = ("y_hi", "core")
FIRST = (4, 3)
SECOND = (1, 2)
THIRD = (1, 4)
FOURTH = (0, 4)
HALF = 64
LANES = 128
HEADS_VMEM = 56
CUTS = 3
GELU_SCALE = 0.7978845608028654
GELU_CUBIC = 0.044715


def place(block, role):
    z = block // 16
    y_hi = (role // 2) ^ (z & 1)
    return block * 4 + y_hi * 2 + role % 2


def move(value, steps):
    pairs = [
        (place(block, role), place((block + (1 - role // 2 * 2) * steps[role % 2]) % 256, role))
        for block in range(256)
        for role in range(4)
        if steps[role % 2]
    ]
    return lax.ppermute(value, AXES, pairs)


def dot(left, right, left_dim, right_dim):
    return lax.dot_general(
        left, right, (((left_dim,), (right_dim,)), ((), ())), preferred_element_type=jnp.float32
    )


def here():
    flip = lax.axis_index("z") & 1
    return lax.axis_index("core"), lax.axis_index("y_hi") ^ flip, flip


def own_half(array, core):
    return array[pl.ds(pl.multiple_of(core * HALF, HALF), HALF), :]


def heads_kernel(
    texts_hbm, head_hbm, images_hbm, fc_in_hbm, fc_out_hbm,
    slope_hbm, kept_ref, sent_ref,
    slope_ref, texts_ref, head_ref, images_ref, fc_in_ref, fc_out_ref, image_term, text_term, sems,
):
    core, unused, unused = here()
    width = images_ref.shape[1]
    cuts = [pl.ds(first, width // CUTS) for first in range(0, width, width // CUTS)]
    pairs = [(texts_hbm, texts_ref), (head_hbm, head_ref), (images_hbm, images_ref)]
    for source, target in ((fc_in_hbm, fc_in_ref), (fc_out_hbm, fc_out_ref)):
        pairs += [(source.at[:, cut], target.at[:, cut]) for cut in cuts]
    copies = [
        pltpu.make_async_copy(source, target, sems.at[index])
        for index, (source, target) in enumerate(pairs)
    ]
    for copy in copies:
        copy.start()
    for copy in copies[:2]:
        copy.wait()
    text_term[...] = dot(texts_ref[...], head_ref[...], 0, 0)
    copies[2].wait()
    pre_act = None
    for cut, copy in zip(cuts, copies[3 : 3 + CUTS]):
        copy.wait()
        part = dot(fc_in_ref[:, cut], images_ref[:, cut], 1, 1)
        pre_act = part if pre_act is None else pre_act + part
    square = pre_act * pre_act
    bent = jnp.tanh(GELU_SCALE * pre_act * (1.0 + GELU_CUBIC * square))
    activation = (0.5 * pre_act * (1.0 + bent)).astype(jnp.bfloat16)
    slope_ref[...] = 0.5 * (1.0 + bent) + (
        0.5 * GELU_SCALE * pre_act * (1.0 - bent * bent) * (1.0 + 3.0 * GELU_CUBIC * square)
    )
    slope_copy = pltpu.make_async_copy(slope_ref, slope_hbm, sems.at[len(copies)])
    slope_copy.start()
    for cut, copy in zip(cuts, copies[3 + CUTS :]):
        copy.wait()
        image_term[:, cut] = dot(activation, fc_out_ref[:, cut], 0, 0)
    for first, term in ((0, image_term), (HALF, text_term)):
        kept_ref[first : first + HALF] = own_half(term, core).astype(jnp.bfloat16)
        sent_ref[first : first + HALF] = own_half(term, 1 - core).astype(jnp.bfloat16)
    slope_copy.wait()


def core_sum_kernel(kept_ref, swapped_ref, sum_ref):
    core, unused, unused = here()
    got = swapped_ref[1 - core].astype(jnp.float32)
    sum_ref[...] = (kept_ref[...].astype(jnp.float32) + got).astype(jnp.bfloat16)


def unit_kernel(
    chips_ref, images_ref, unit_ref, inverse_ref, own_sent_ref, moved_sent_ref
):
    core, side, unused = here()
    embed = chips_ref[0].astype(jnp.float32) + chips_ref[1].astype(jnp.float32)
    image_embed = own_half(images_ref, core).astype(jnp.float32) + embed[:HALF]
    units = []
    for first, rows in ((0, image_embed), (HALF, embed[HALF:])):
        inverse = lax.rsqrt(jnp.sum(rows * rows, axis=1, keepdims=True) + epsilon)
        units.append(rows * inverse)
        unit_ref[first : first + HALF] = units[-1]
        inverse_ref[first : first + HALF] = jnp.broadcast_to(inverse, (HALF, LANES))
    own_sent_ref[...] = jnp.where(side == 0, units[0], units[1]).astype(jnp.bfloat16)
    moved_sent_ref[...] = jnp.where(side == 0, units[1], units[0]).astype(jnp.bfloat16)


def split_loss(loss):
    high = loss.astype(jnp.bfloat16).astype(jnp.float32)
    lanes = lax.broadcasted_iota(jnp.int32, (loss.shape[0], LANES), 1)
    return jnp.where(lanes == 0, high, jnp.where(lanes == 1, loss - high, 0.0))


def pair_terms(own, others, positive):
    logits = logit_scale * dot(own, others, 1, 1) + logit_bias
    if positive is None:
        flipped = logits
    else:
        flipped = jnp.where(positive, -logits, logits)
    small = jnp.exp(-jnp.abs(flipped))
    loss = jnp.maximum(flipped, 0.0) + jnp.log1p(small)
    sigmoid = jnp.where(flipped >= 0.0, 1.0, small) / (1.0 + small)
    if positive is None:
        pair_grad = loss_scale * sigmoid
    else:
        pair_grad = jnp.where(positive, -loss_scale, loss_scale) * sigmoid
    return logit_scale * dot(pair_grad.astype(jnp.bfloat16), others, 1, 0), loss


def early_kernel(own_ref, first_ref, second_ref, part_ref):
    rows, width = own_ref.shape
    own = own_ref[...]
    first, first_loss = pair_terms(own, first_ref[...], None)
    second, second_loss = pair_terms(own, second_ref[...], None)
    part_ref[:, :width] = first + second
    loss = jnp.sum(first_loss + second_loss, axis=1, keepdims=True)
    part_ref[:, width:] = jnp.broadcast_to(loss, (rows, LANES))


def late_kernel(
    own_ref, moved_ref, third_ref, fourth_ref, column_ref, row_ref, early_ref,
    kept_ref, sent_ref, part_ref,
):
    core, side, unused = here()
    rows, width = own_ref.shape
    own = own_ref[...]
    across = lax.broadcasted_iota(jnp.int32, (rows, rows), 1) == column_ref[...]
    down = lax.broadcasted_iota(jnp.int32, (rows, rows), 0) == row_ref[...]
    paired = jnp.where(side == 0, across.astype(jnp.int32), down.astype(jnp.int32))
    third, third_loss = pair_terms(own, third_ref[...], None)
    last = jnp.where(core == 0, moved_ref[...], fourth_ref[...])
    last, last_loss = pair_terms(own, last, paired == 1)
    part_ref[:, :width] = early_ref[:, :width] + third + last
    loss = jnp.sum(third_loss + last_loss, axis=1, keepdims=True)
    part_ref[:, width:] = split_loss(early_ref[:, width : width + 1] + loss)
    kept_ref[...] = own_half(part_ref, core)
    sent_ref[...] = own_half(part_ref, 1 - core).astype(jnp.bfloat16)


def tangent_kernel(kept_ref, swapped_ref, unit_ref, inverse_ref, sent_ref):
    width = unit_ref.shape[1]
    core, side, unused = here()
    sums = kept_ref[...] + swapped_ref[1 - core].astype(jnp.float32)
    side = pl.ds(pl.multiple_of(side * HALF, HALF), HALF)
    grad, unit = sums[:, :width], unit_ref[side, :]
    along = jnp.sum(unit * grad, axis=1, keepdims=True)
    tangent = (grad - unit * along) * inverse_ref[side, :][:, :1]
    sent_ref[:, :width] = tangent.astype(jnp.bfloat16)
    loss = sums[:, width : width + 1] + sums[:, width + 1 : width + 2]
    sent_ref[:, width:] = split_loss(loss).astype(jnp.bfloat16)


def backward_kernel(
    grads_ref, slope_ref, fc_out_ref, head_ref, hidden_ref, text_ref, loss_ref
):
    rows, width = 2 * HALF, fc_out_ref.shape[1]
    unused, unused, flip = here()
    image_chip = flip * 2
    image_grad = grads_ref[pl.ds(image_chip, 2)].reshape(rows, width + LANES)
    text_grad = grads_ref[pl.ds(2 - image_chip, 2)].reshape(rows, width + LANES)
    losses = jnp.sum(image_grad[:, width:].astype(jnp.float32), axis=1, keepdims=True)
    loss_ref[...] = jnp.broadcast_to(losses, (rows, LANES)).T[:1] / (WINDOW * rows)
    act_grad = dot(fc_out_ref[...], image_grad[:, :width], 1, 1)
    hidden_ref[...] = (slope_ref[...] * act_grad).astype(jnp.bfloat16)
    text_ref[...] = dot(head_ref[...], text_grad[:, :width], 1, 1).astype(jnp.bfloat16)


def kernel(body, outs, scratch=(), places="", vmem=24, out_places=None):
    spaces = dict(v=pltpu.VMEM, h=pltpu.HBM)
    return pl.pallas_call(
        body,
        out_shape=[jax.ShapeDtypeStruct(shape, dtype) for shape, dtype in outs],
        in_specs=[pl.BlockSpec(memory_space=spaces[place]) for place in places],
        out_specs=[
            pl.BlockSpec(memory_space=spaces[place]) for place in out_places or "v" * len(outs)
        ],
        scratch_shapes=list(scratch),
        compiler_params=pltpu.CompilerParams(vmem_limit_bytes=vmem * 1024 * 1024),
    )


def local(images, texts, fc_in, fc_out, head, partner):
    rows, width = images.shape
    hidden, features = fc_out.shape[0], head.shape[0]
    f32, bf16 = jnp.float32, jnp.bfloat16
    slope, kept, sent = kernel(
        heads_kernel,
        [((hidden, rows), f32), ((rows, width), bf16), ((rows, width), bf16)],
        [
            pltpu.VMEM((hidden, rows), f32),
            pltpu.VMEM((features, rows), bf16),
            pltpu.VMEM((features, width), bf16),
            pltpu.VMEM((rows, width), bf16),
            pltpu.VMEM((hidden, width), bf16),
            pltpu.VMEM((hidden, width), bf16),
            pltpu.VMEM((rows, width), f32),
            pltpu.VMEM((rows, width), f32),
            pltpu.SemaphoreType.DMA((4 + 2 * CUTS,)),
        ],
        "hhhhh",
        vmem=HEADS_VMEM,
        out_places="hvv",
    )(texts.T, head, images, fc_in.T, fc_out)
    (core_sum,) = kernel(core_sum_kernel, [((rows, width), bf16)], places="vv")(
        kept, lax.all_gather(sent, "core")
    )
    chips = lax.all_gather(core_sum, "y_hi")

    unit, inverse, own_sent, moved_sent = kernel(
        unit_kernel,
        [((rows, width), f32), ((rows, LANES), f32)] + [((HALF, width), bf16)] * 2,
        places="vv",
    )(chips, images)

    moved = lax.all_gather(moved_sent, "core", tiled=True)
    moved, own_sent = lax.optimization_barrier((moved, own_sent))
    first = move(moved, FIRST)
    second = move(moved, SECOND)
    own = lax.all_gather(own_sent, "core", tiled=True)
    third = move(first, THIRD)
    fourth = move(second, FOURTH)

    paired = jnp.where(lax.axis_index("core") == 0, partner, -1)
    columns = width + LANES
    part = [((rows, columns), f32)]
    (early,) = kernel(early_kernel, part, places="vvv")(own, first, second)
    kept, sent = kernel(
        late_kernel,
        [((HALF, columns), f32), ((HALF, columns), bf16)],
        [pltpu.VMEM(*part[0])],
        "vvvvvvv",
    )(own, moved, third, fourth, paired.reshape(rows, 1), paired.reshape(1, rows), early)

    (grads,) = kernel(tangent_kernel, [((HALF, columns), bf16)], places="vvvv")(
        kept, lax.all_gather(sent, "core"), unit, inverse
    )
    hidden_grad, text_grad, loss = kernel(
        backward_kernel,
        [((hidden, rows), bf16), ((features, rows), bf16), ((1, rows), f32)],
        places="vvvv",
    )(lax.all_gather(grads, MP), slope, fc_out, head)
    return (hidden_grad.T, text_grad.T, loss.reshape(rows))


def solution(mesh):
    dp = ("z", "y_lo", "x")
    return jax.shard_map(
        local,
        mesh=Mesh(mesh.devices.reshape(SIZES), AXES),
        in_specs=(P(dp, None), P(dp, MP), P(None, MP), P(MP, None), P(MP, None), P(dp)),
        out_specs=(P(dp, MP), P(dp, MP), P(dp)),
        check_vma=False,
    )
```

```python
import jax
import jax.numpy as jnp
from jax import lax
from jax.experimental import pallas as pl
from jax.experimental.pallas import tpu as pltpu
from jax.sharding import Mesh, PartitionSpec as P

WINDOW = 8


logit_scale = 32.0
logit_bias = -2.0
loss_scale = 16.0
epsilon = 1e-06

AXES = ("z", "y_lo", "x", "y_hi", "core")
SIZES = (16, 4, 4, 2, 2)
MP = ("y_hi", "core")
FIRST = (1, 3)
SECOND = (4, 2)
RELAY = 4
HALF = 64
LANES = 128
HEADS_VMEM = 56
CUTS = 3
GELU_SCALE = 0.7978845608028654
GELU_CUBIC = 0.044715


def place(block, role):
    z = block // 16
    y_hi = (role // 2) ^ (z & 1)
    return block * 4 + y_hi * 2 + role % 2


def move(value, steps):
    pairs = [
        (place(block, role), place((block + (1 - role // 2 * 2) * steps[role % 2]) % 256, role))
        for block in range(256)
        for role in range(4)
        if steps[role % 2]
    ]
    return lax.ppermute(value, AXES, pairs)


def dot(left, right, left_dim, right_dim):
    return lax.dot_general(
        left, right, (((left_dim,), (right_dim,)), ((), ())), preferred_element_type=jnp.float32
    )


def here():
    flip = lax.axis_index("z") & 1
    return lax.axis_index("core"), lax.axis_index("y_hi") ^ flip, flip


def own_half(array, core):
    return array[pl.ds(pl.multiple_of(core * HALF, HALF), HALF), :]


def heads_kernel(
    texts_hbm, head_hbm, images_hbm, fc_in_hbm, fc_out_hbm,
    slope_hbm, kept_ref, sent_ref,
    slope_ref, texts_ref, head_ref, images_ref, fc_in_ref, fc_out_ref, image_term, text_term, sems,
):
    core, unused, unused = here()
    width = images_ref.shape[1]
    cuts = [pl.ds(first, width // CUTS) for first in range(0, width, width // CUTS)]
    pairs = [(texts_hbm, texts_ref), (head_hbm, head_ref), (images_hbm, images_ref)]
    for source, target in ((fc_in_hbm, fc_in_ref), (fc_out_hbm, fc_out_ref)):
        pairs += [(source.at[:, cut], target.at[:, cut]) for cut in cuts]
    copies = [
        pltpu.make_async_copy(source, target, sems.at[index])
        for index, (source, target) in enumerate(pairs)
    ]
    for copy in copies:
        copy.start()
    for copy in copies[:2]:
        copy.wait()
    text_term[...] = dot(texts_ref[...], head_ref[...], 0, 0)
    copies[2].wait()
    pre_act = None
    for cut, copy in zip(cuts, copies[3 : 3 + CUTS]):
        copy.wait()
        part = dot(fc_in_ref[:, cut], images_ref[:, cut], 1, 1)
        pre_act = part if pre_act is None else pre_act + part
    square = pre_act * pre_act
    bent = jnp.tanh(GELU_SCALE * pre_act * (1.0 + GELU_CUBIC * square))
    activation = (0.5 * pre_act * (1.0 + bent)).astype(jnp.bfloat16)
    slope_ref[...] = 0.5 * (1.0 + bent) + (
        0.5 * GELU_SCALE * pre_act * (1.0 - bent * bent) * (1.0 + 3.0 * GELU_CUBIC * square)
    )
    slope_copy = pltpu.make_async_copy(slope_ref, slope_hbm, sems.at[len(copies)])
    slope_copy.start()
    for cut, copy in zip(cuts, copies[3 + CUTS :]):
        copy.wait()
        image_term[:, cut] = dot(activation, fc_out_ref[:, cut], 0, 0)
    for first, term in ((0, image_term), (HALF, text_term)):
        kept_ref[first : first + HALF] = own_half(term, core).astype(jnp.bfloat16)
        sent_ref[first : first + HALF] = own_half(term, 1 - core).astype(jnp.bfloat16)
    slope_copy.wait()


def core_sum_kernel(kept_ref, swapped_ref, own_ref, moved_ref):
    core, side, unused = here()
    got = swapped_ref[1 - core].astype(jnp.float32)
    sums = (kept_ref[...].astype(jnp.float32) + got).astype(jnp.bfloat16)
    own_ref[...] = jnp.where(side == 0, sums[:HALF], sums[HALF:])
    moved_ref[...] = jnp.where(side == 0, sums[HALF:], sums[:HALF])


def embed_rows(chip_ref, other_ref, images_ref, image_side):
    core, side, unused = here()
    residual = own_half(images_ref, core).astype(jnp.float32)
    sums = chip_ref[...].astype(jnp.float32) + other_ref[...].astype(jnp.float32)
    return sums + jnp.where(side == image_side, residual, 0.0)


def moved_unit_kernel(chip_ref, other_ref, images_ref, sent_ref):
    rows = embed_rows(chip_ref, other_ref, images_ref, 1)
    inverse = lax.rsqrt(jnp.sum(rows * rows, axis=1, keepdims=True) + epsilon)
    sent_ref[...] = (rows * inverse).astype(jnp.bfloat16)


def own_unit_kernel(chip_ref, other_ref, images_ref, unit_ref, inverse_ref, sent_ref):
    rows = embed_rows(chip_ref, other_ref, images_ref, 0)
    inverse = lax.rsqrt(jnp.sum(rows * rows, axis=1, keepdims=True) + epsilon)
    unit_ref[...] = rows * inverse
    inverse_ref[...] = jnp.broadcast_to(inverse, (HALF, LANES))
    sent_ref[...] = (rows * inverse).astype(jnp.bfloat16)


def split_loss(loss):
    high = loss.astype(jnp.bfloat16).astype(jnp.float32)
    lanes = lax.broadcasted_iota(jnp.int32, (loss.shape[0], LANES), 1)
    return jnp.where(lanes == 0, high, jnp.where(lanes == 1, loss - high, 0.0))


def pair_terms(own, others, positive):
    logits = logit_scale * dot(own, others, 1, 1) + logit_bias
    if positive is None:
        flipped = logits
    else:
        flipped = jnp.where(positive, -logits, logits)
    small = jnp.exp(-jnp.abs(flipped))
    loss = jnp.maximum(flipped, 0.0) + jnp.log1p(small)
    sigmoid = jnp.where(flipped >= 0.0, 1.0, small) / (1.0 + small)
    if positive is None:
        pair_grad = loss_scale * sigmoid
    else:
        pair_grad = jnp.where(positive, -loss_scale, loss_scale) * sigmoid
    return logit_scale * dot(pair_grad.astype(jnp.bfloat16), others, 1, 0), loss


def early_kernel(own_ref, first_ref, second_ref, part_ref):
    rows, width = own_ref.shape
    own = own_ref[...]
    first, first_loss = pair_terms(own, first_ref[...], None)
    second, second_loss = pair_terms(own, second_ref[...], None)
    part_ref[:, :width] = first + second
    loss = jnp.sum(first_loss + second_loss, axis=1, keepdims=True)
    part_ref[:, width:] = jnp.broadcast_to(loss, (rows, LANES))


def late_kernel(
    own_ref, moved_ref, third_ref, fourth_ref, column_ref, row_ref, early_ref,
    kept_ref, sent_ref, part_ref,
):
    core, side, unused = here()
    rows, width = own_ref.shape
    own = own_ref[...]
    across = lax.broadcasted_iota(jnp.int32, (rows, rows), 1) == column_ref[...]
    down = lax.broadcasted_iota(jnp.int32, (rows, rows), 0) == row_ref[...]
    paired = jnp.where(side == 0, across.astype(jnp.int32), down.astype(jnp.int32))
    third, third_loss = pair_terms(own, third_ref[...], None)
    last = jnp.where(core == 0, moved_ref[...], fourth_ref[...])
    last, last_loss = pair_terms(own, last, paired == 1)
    part_ref[:, :width] = early_ref[:, :width] + third + last
    loss = jnp.sum(third_loss + last_loss, axis=1, keepdims=True)
    part_ref[:, width:] = split_loss(early_ref[:, width : width + 1] + loss)
    kept_ref[...] = own_half(part_ref, core)
    sent_ref[...] = own_half(part_ref, 1 - core).astype(jnp.bfloat16)


def tangent_kernel(kept_ref, swapped_ref, unit_ref, inverse_ref, sent_ref):
    width = unit_ref.shape[1]
    core, unused, unused = here()
    sums = kept_ref[...] + swapped_ref[1 - core].astype(jnp.float32)
    grad, unit = sums[:, :width], unit_ref[...]
    along = jnp.sum(unit * grad, axis=1, keepdims=True)
    tangent = (grad - unit * along) * inverse_ref[:, :1]
    sent_ref[:, :width] = tangent.astype(jnp.bfloat16)
    loss = sums[:, width : width + 1] + sums[:, width + 1 : width + 2]
    sent_ref[:, width:] = split_loss(loss).astype(jnp.bfloat16)


def backward_kernel(
    grads_ref, slope_ref, fc_out_ref, head_ref, hidden_ref, text_ref, loss_ref
):
    rows, width = 2 * HALF, fc_out_ref.shape[1]
    unused, unused, flip = here()
    image_chip = flip * 2
    image_grad = grads_ref[pl.ds(image_chip, 2)].reshape(rows, width + LANES)
    text_grad = grads_ref[pl.ds(2 - image_chip, 2)].reshape(rows, width + LANES)
    losses = jnp.sum(image_grad[:, width:].astype(jnp.float32), axis=1, keepdims=True)
    loss_ref[...] = jnp.broadcast_to(losses, (rows, LANES)).T[:1] / (WINDOW * rows)
    act_grad = dot(fc_out_ref[...], image_grad[:, :width], 1, 1)
    hidden_ref[...] = (slope_ref[...] * act_grad).astype(jnp.bfloat16)
    text_ref[...] = dot(head_ref[...], text_grad[:, :width], 1, 1).astype(jnp.bfloat16)


def kernel(body, outs, scratch=(), places="", vmem=24, out_places=None):
    spaces = dict(v=pltpu.VMEM, h=pltpu.HBM)
    return pl.pallas_call(
        body,
        out_shape=[jax.ShapeDtypeStruct(shape, dtype) for shape, dtype in outs],
        in_specs=[pl.BlockSpec(memory_space=spaces[place]) for place in places],
        out_specs=[
            pl.BlockSpec(memory_space=spaces[place]) for place in out_places or "v" * len(outs)
        ],
        scratch_shapes=list(scratch),
        compiler_params=pltpu.CompilerParams(vmem_limit_bytes=vmem * 1024 * 1024),
    )


def local(images, texts, fc_in, fc_out, head, partner):
    rows, width = images.shape
    hidden, features = fc_out.shape[0], head.shape[0]
    f32, bf16 = jnp.float32, jnp.bfloat16
    slope, kept, sent = kernel(
        heads_kernel,
        [((hidden, rows), f32), ((rows, width), bf16), ((rows, width), bf16)],
        [
            pltpu.VMEM((hidden, rows), f32),
            pltpu.VMEM((features, rows), bf16),
            pltpu.VMEM((features, width), bf16),
            pltpu.VMEM((rows, width), bf16),
            pltpu.VMEM((hidden, width), bf16),
            pltpu.VMEM((hidden, width), bf16),
            pltpu.VMEM((rows, width), f32),
            pltpu.VMEM((rows, width), f32),
            pltpu.SemaphoreType.DMA((4 + 2 * CUTS,)),
        ],
        "hhhhh",
        vmem=HEADS_VMEM,
        out_places="hvv",
    )(texts.T, head, images, fc_in.T, fc_out)
    half = ((HALF, width), bf16)
    own_chip, moved_chip = kernel(core_sum_kernel, [half, half], places="vv")(
        kept, lax.all_gather(sent, "core")
    )
    moved_other = lax.ppermute(own_chip, "y_hi", [(0, 1), (1, 0)])
    own_other = lax.ppermute(moved_chip, "y_hi", [(0, 1), (1, 0)])
    (moved_sent,) = kernel(moved_unit_kernel, [half], places="vvv")(
        moved_chip, moved_other, images
    )
    moved = lax.all_gather(moved_sent, "core", tiled=True)
    first = move(moved, FIRST)
    second = move(moved, SECOND)
    unit, inverse, own_sent = kernel(
        own_unit_kernel, [((HALF, width), f32), ((HALF, LANES), f32), half], places="vvv"
    )(own_chip, own_other, images)
    own = lax.all_gather(own_sent, "core", tiled=True)
    third = move(first, (RELAY, RELAY))
    fourth = move(second, (0, RELAY))

    paired = jnp.where(lax.axis_index("core") == 0, partner, -1)
    columns = width + LANES
    part = [((rows, columns), f32)]
    (early,) = kernel(early_kernel, part, places="vvv")(own, first, second)
    kept, sent = kernel(
        late_kernel,
        [((HALF, columns), f32), ((HALF, columns), bf16)],
        [pltpu.VMEM(*part[0])],
        "vvvvvvv",
    )(own, moved, third, fourth, paired.reshape(rows, 1), paired.reshape(1, rows), early)

    (grads,) = kernel(tangent_kernel, [((HALF, columns), bf16)], places="vvvv")(
        kept, lax.all_gather(sent, "core"), unit, inverse
    )
    hidden_grad, text_grad, loss = kernel(
        backward_kernel,
        [((hidden, rows), bf16), ((features, rows), bf16), ((1, rows), f32)],
        places="vvvv",
    )(lax.all_gather(grads, MP), slope, fc_out, head)
    return (hidden_grad.T, text_grad.T, loss.reshape(rows))


def solution(mesh):
    dp = ("z", "y_lo", "x")
    return jax.shard_map(
        local,
        mesh=Mesh(mesh.devices.reshape(SIZES), AXES),
        in_specs=(P(dp, None), P(dp, MP), P(None, MP), P(MP, None), P(MP, None), P(dp)),
        out_specs=(P(dp, MP), P(dp, MP), P(dp)),
        check_vma=False,
    )
```

```python
import jax
import jax.numpy as jnp
from jax import lax
from jax.experimental import pallas as pl
from jax.experimental.pallas import tpu as pltpu
from jax.sharding import Mesh, PartitionSpec as P

WINDOW = 8


logit_scale = 32.0
logit_bias = -2.0
loss_scale = 16.0
epsilon = 1e-06

AXES = ("z", "y_lo", "x", "y_hi", "core")
SIZES = (16, 4, 4, 2, 2)
MP = ("y_hi", "core")
FIRST = (4, 3)
SECOND = (1, 2)
THIRD = (1, 4)
FOURTH = (2, 0)
HALF = 64
LANES = 128
HEADS_VMEM = 56
CUTS = 3
GELU_SCALE = 0.7978845608028654
GELU_CUBIC = 0.044715


def place(block, role):
    z = block // 16
    y_hi = (role // 2) ^ (z & 1)
    return block * 4 + y_hi * 2 + role % 2


def move(value, steps):
    pairs = [
        (place(block, role), place((block + (1 - role // 2 * 2) * steps[role % 2]) % 256, role))
        for block in range(256)
        for role in range(4)
        if steps[role % 2]
    ]
    return lax.ppermute(value, AXES, pairs)


def dot(left, right, left_dim, right_dim):
    return lax.dot_general(
        left, right, (((left_dim,), (right_dim,)), ((), ())), preferred_element_type=jnp.float32
    )


def here():
    flip = lax.axis_index("z") & 1
    return lax.axis_index("core"), lax.axis_index("y_hi") ^ flip, flip


def own_half(array, core):
    return array[pl.ds(pl.multiple_of(core * HALF, HALF), HALF), :]


def heads_kernel(
    texts_hbm, head_hbm, images_hbm, fc_in_hbm, fc_out_hbm,
    slope_hbm, kept_ref, sent_ref,
    slope_ref, texts_ref, head_ref, images_ref, fc_in_ref, fc_out_ref, image_term, text_term, sems,
):
    core, unused, unused = here()
    width = images_ref.shape[1]
    cuts = [pl.ds(first, width // CUTS) for first in range(0, width, width // CUTS)]
    pairs = [(texts_hbm, texts_ref), (head_hbm, head_ref), (images_hbm, images_ref)]
    for source, target in ((fc_in_hbm, fc_in_ref), (fc_out_hbm, fc_out_ref)):
        pairs += [(source.at[:, cut], target.at[:, cut]) for cut in cuts]
    copies = [
        pltpu.make_async_copy(source, target, sems.at[index])
        for index, (source, target) in enumerate(pairs)
    ]
    for copy in copies:
        copy.start()
    for copy in copies[:2]:
        copy.wait()
    text_term[...] = dot(texts_ref[...], head_ref[...], 0, 0)
    copies[2].wait()
    pre_act = None
    for cut, copy in zip(cuts, copies[3 : 3 + CUTS]):
        copy.wait()
        part = dot(fc_in_ref[:, cut], images_ref[:, cut], 1, 1)
        pre_act = part if pre_act is None else pre_act + part
    square = pre_act * pre_act
    bent = jnp.tanh(GELU_SCALE * pre_act * (1.0 + GELU_CUBIC * square))
    activation = (0.5 * pre_act * (1.0 + bent)).astype(jnp.bfloat16)
    slope_ref[...] = 0.5 * (1.0 + bent) + (
        0.5 * GELU_SCALE * pre_act * (1.0 - bent * bent) * (1.0 + 3.0 * GELU_CUBIC * square)
    )
    slope_copy = pltpu.make_async_copy(slope_ref, slope_hbm, sems.at[len(copies)])
    slope_copy.start()
    for cut, copy in zip(cuts, copies[3 + CUTS :]):
        copy.wait()
        image_term[:, cut] = dot(activation, fc_out_ref[:, cut], 0, 0)
    for first, term in ((0, image_term), (HALF, text_term)):
        kept_ref[first : first + HALF] = own_half(term, core).astype(jnp.bfloat16)
        sent_ref[first : first + HALF] = own_half(term, 1 - core).astype(jnp.bfloat16)
    slope_copy.wait()


def core_sum_kernel(kept_ref, swapped_ref, own_ref, moved_ref):
    core, side, unused = here()
    got = swapped_ref[1 - core].astype(jnp.float32)
    sums = (kept_ref[...].astype(jnp.float32) + got).astype(jnp.bfloat16)
    own_ref[...] = jnp.where(side == 0, sums[:HALF], sums[HALF:])
    moved_ref[...] = jnp.where(side == 0, sums[HALF:], sums[:HALF])


def embed_rows(chip_ref, other_ref, images_ref, image_side):
    core, side, unused = here()
    residual = own_half(images_ref, core).astype(jnp.float32)
    sums = chip_ref[...].astype(jnp.float32) + other_ref[...].astype(jnp.float32)
    return sums + jnp.where(side == image_side, residual, 0.0)


def moved_unit_kernel(chip_ref, other_ref, images_ref, sent_ref):
    rows = embed_rows(chip_ref, other_ref, images_ref, 1)
    inverse = lax.rsqrt(jnp.sum(rows * rows, axis=1, keepdims=True) + epsilon)
    sent_ref[...] = (rows * inverse).astype(jnp.bfloat16)


def own_unit_kernel(chip_ref, other_ref, images_ref, unit_ref, inverse_ref, sent_ref):
    rows = embed_rows(chip_ref, other_ref, images_ref, 0)
    inverse = lax.rsqrt(jnp.sum(rows * rows, axis=1, keepdims=True) + epsilon)
    unit_ref[...] = rows * inverse
    inverse_ref[...] = jnp.broadcast_to(inverse, (HALF, LANES))
    sent_ref[...] = (rows * inverse).astype(jnp.bfloat16)


def split_loss(loss):
    high = loss.astype(jnp.bfloat16).astype(jnp.float32)
    lanes = lax.broadcasted_iota(jnp.int32, (loss.shape[0], LANES), 1)
    return jnp.where(lanes == 0, high, jnp.where(lanes == 1, loss - high, 0.0))


def pair_terms(own, others, positive, weight=1.0):
    logits = logit_scale * dot(own, others, 1, 1) + logit_bias
    if positive is None:
        flipped = logits
    else:
        flipped = jnp.where(positive, -logits, logits)
    small = jnp.exp(-jnp.abs(flipped))
    loss = weight * (jnp.maximum(flipped, 0.0) + jnp.log1p(small))
    sigmoid = jnp.where(flipped >= 0.0, 1.0, small) / (1.0 + small)
    if positive is None:
        pair_grad = weight * loss_scale * sigmoid
    else:
        pair_grad = weight * jnp.where(positive, -loss_scale, loss_scale) * sigmoid
    return logit_scale * dot(pair_grad.astype(jnp.bfloat16), others, 1, 0), loss


def early_kernel(own_ref, first_ref, second_ref, part_ref):
    rows, width = own_ref.shape
    own = own_ref[...]
    first, first_loss = pair_terms(own, first_ref[...], None)
    second, second_loss = pair_terms(own, second_ref[...], None)
    part_ref[:, :width] = first + second
    loss = jnp.sum(first_loss + second_loss, axis=1, keepdims=True)
    part_ref[:, width:] = jnp.broadcast_to(loss, (rows, LANES))


def late_kernel(
    own_ref, moved_ref, third_ref, fourth_ref, column_ref, row_ref, early_ref,
    kept_ref, sent_ref, part_ref,
):
    core, side, unused = here()
    rows, width = own_ref.shape
    own = own_ref[...]
    across = lax.broadcasted_iota(jnp.int32, (rows, rows), 1) == column_ref[...]
    down = lax.broadcasted_iota(jnp.int32, (rows, rows), 0) == row_ref[...]
    paired = jnp.where(side == 0, across.astype(jnp.int32), down.astype(jnp.int32))
    third, third_loss = pair_terms(own, third_ref[...], None)
    weight = jnp.where(core == 0, 1.0, 0.0)
    fourth, fourth_loss = pair_terms(own, fourth_ref[...], None, weight)
    near, near_loss = pair_terms(own, moved_ref[...], paired == 1, weight)
    part_ref[:, :width] = early_ref[:, :width] + third + fourth + near
    loss = jnp.sum(third_loss + fourth_loss + near_loss, axis=1, keepdims=True)
    part_ref[:, width:] = split_loss(early_ref[:, width : width + 1] + loss)
    kept_ref[...] = own_half(part_ref, core)
    sent_ref[...] = own_half(part_ref, 1 - core).astype(jnp.bfloat16)


def tangent_kernel(kept_ref, swapped_ref, unit_ref, inverse_ref, sent_ref):
    width = unit_ref.shape[1]
    core, unused, unused = here()
    sums = kept_ref[...] + swapped_ref[1 - core].astype(jnp.float32)
    grad, unit = sums[:, :width], unit_ref[...]
    along = jnp.sum(unit * grad, axis=1, keepdims=True)
    tangent = (grad - unit * along) * inverse_ref[:, :1]
    sent_ref[:, :width] = tangent.astype(jnp.bfloat16)
    loss = sums[:, width : width + 1] + sums[:, width + 1 : width + 2]
    sent_ref[:, width:] = split_loss(loss).astype(jnp.bfloat16)


def backward_kernel(
    grads_ref, slope_ref, fc_out_ref, head_ref, hidden_ref, text_ref, loss_ref
):
    rows, width = 2 * HALF, fc_out_ref.shape[1]
    unused, unused, flip = here()
    image_chip = flip * 2
    image_grad = grads_ref[pl.ds(image_chip, 2)].reshape(rows, width + LANES)
    text_grad = grads_ref[pl.ds(2 - image_chip, 2)].reshape(rows, width + LANES)
    losses = jnp.sum(image_grad[:, width:].astype(jnp.float32), axis=1, keepdims=True)
    loss_ref[...] = jnp.broadcast_to(losses, (rows, LANES)).T[:1] / (WINDOW * rows)
    act_grad = dot(fc_out_ref[...], image_grad[:, :width], 1, 1)
    hidden_ref[...] = (slope_ref[...] * act_grad).astype(jnp.bfloat16)
    text_ref[...] = dot(head_ref[...], text_grad[:, :width], 1, 1).astype(jnp.bfloat16)


def kernel(body, outs, scratch=(), places="", vmem=24, out_places=None):
    spaces = dict(v=pltpu.VMEM, h=pltpu.HBM)
    return pl.pallas_call(
        body,
        out_shape=[jax.ShapeDtypeStruct(shape, dtype) for shape, dtype in outs],
        in_specs=[pl.BlockSpec(memory_space=spaces[place]) for place in places],
        out_specs=[
            pl.BlockSpec(memory_space=spaces[place]) for place in out_places or "v" * len(outs)
        ],
        scratch_shapes=list(scratch),
        compiler_params=pltpu.CompilerParams(vmem_limit_bytes=vmem * 1024 * 1024),
    )


def local(images, texts, fc_in, fc_out, head, partner):
    rows, width = images.shape
    hidden, features = fc_out.shape[0], head.shape[0]
    f32, bf16 = jnp.float32, jnp.bfloat16
    slope, kept, sent = kernel(
        heads_kernel,
        [((hidden, rows), f32), ((rows, width), bf16), ((rows, width), bf16)],
        [
            pltpu.VMEM((hidden, rows), f32),
            pltpu.VMEM((features, rows), bf16),
            pltpu.VMEM((features, width), bf16),
            pltpu.VMEM((rows, width), bf16),
            pltpu.VMEM((hidden, width), bf16),
            pltpu.VMEM((hidden, width), bf16),
            pltpu.VMEM((rows, width), f32),
            pltpu.VMEM((rows, width), f32),
            pltpu.SemaphoreType.DMA((4 + 2 * CUTS,)),
        ],
        "hhhhh",
        vmem=HEADS_VMEM,
        out_places="hvv",
    )(texts.T, head, images, fc_in.T, fc_out)
    half = ((HALF, width), bf16)
    own_chip, moved_chip = kernel(core_sum_kernel, [half, half], places="vv")(
        kept, lax.all_gather(sent, "core")
    )
    moved_other = lax.ppermute(own_chip, "y_hi", [(0, 1), (1, 0)])
    own_other = lax.ppermute(moved_chip, "y_hi", [(0, 1), (1, 0)])
    (moved_sent,) = kernel(moved_unit_kernel, [half], places="vvv")(
        moved_chip, moved_other, images
    )
    moved = lax.all_gather(moved_sent, "core", tiled=True)
    first = move(moved, FIRST)
    second = move(moved, SECOND)
    unit, inverse, own_sent = kernel(
        own_unit_kernel, [((HALF, width), f32), ((HALF, LANES), f32), half], places="vvv"
    )(own_chip, own_other, images)
    own = lax.all_gather(own_sent, "core", tiled=True)
    third = move(first, THIRD)
    fourth = move(first, FOURTH)

    paired = jnp.where(lax.axis_index("core") == 0, partner, -1)
    columns = width + LANES
    part = [((rows, columns), f32)]
    (early,) = kernel(early_kernel, part, places="vvv")(own, first, second)
    kept, sent = kernel(
        late_kernel,
        [((HALF, columns), f32), ((HALF, columns), bf16)],
        [pltpu.VMEM(*part[0])],
        "vvvvvvv",
    )(own, moved, third, fourth, paired.reshape(rows, 1), paired.reshape(1, rows), early)

    (grads,) = kernel(tangent_kernel, [((HALF, columns), bf16)], places="vvvv")(
        kept, lax.all_gather(sent, "core"), unit, inverse
    )
    hidden_grad, text_grad, loss = kernel(
        backward_kernel,
        [((hidden, rows), bf16), ((features, rows), bf16), ((1, rows), f32)],
        places="vvvv",
    )(lax.all_gather(grads, MP), slope, fc_out, head)
    return (hidden_grad.T, text_grad.T, loss.reshape(rows))


def solution(mesh):
    dp = ("z", "y_lo", "x")
    return jax.shard_map(
        local,
        mesh=Mesh(mesh.devices.reshape(SIZES), AXES),
        in_specs=(P(dp, None), P(dp, MP), P(None, MP), P(MP, None), P(MP, None), P(dp)),
        out_specs=(P(dp, MP), P(dp, MP), P(dp)),
        check_vma=False,
    )
```

```python
import jax
import jax.numpy as jnp
from jax import lax
from jax.experimental import pallas as pl
from jax.experimental.pallas import tpu as pltpu
from jax.sharding import Mesh, PartitionSpec as P

WINDOW = 8


logit_scale = 32.0
logit_bias = -2.0
loss_scale = 16.0
epsilon = 1e-06

AXES = ("z", "y_lo", "x", "y_hi", "core")
SIZES = (16, 4, 4, 2, 2)
MP = ("y_hi", "core")
FIRST = (1, 3)
SECOND = (4, 2)
RELAY = 4
HALF = 64
LANES = 128
HEADS_VMEM = 56
CUTS = 3
GELU_SCALE = 0.7978845608028654
GELU_CUBIC = 0.044715


def place(block, role):
    z = block // 16
    y_hi = (role // 2) ^ (z & 1)
    return block * 4 + y_hi * 2 + role % 2


def move(value, steps):
    pairs = [
        (place(block, role), place((block + (1 - role // 2 * 2) * steps[role % 2]) % 256, role))
        for block in range(256)
        for role in range(4)
        if steps[role % 2]
    ]
    return lax.ppermute(value, AXES, pairs)


def dot(left, right, left_dim, right_dim):
    return lax.dot_general(
        left, right, (((left_dim,), (right_dim,)), ((), ())), preferred_element_type=jnp.float32
    )


def here():
    flip = lax.axis_index("z") & 1
    return lax.axis_index("core"), lax.axis_index("y_hi") ^ flip, flip


def own_half(array, core):
    return array[pl.ds(pl.multiple_of(core * HALF, HALF), HALF), :]


def heads_kernel(
    texts_hbm, head_hbm, images_hbm, fc_in_hbm, fc_out_hbm,
    slope_hbm, kept_ref, sent_ref,
    slope_ref, texts_ref, head_ref, images_ref, fc_in_ref, fc_out_ref, image_term, text_term, sems,
):
    core, unused, unused = here()
    width = images_ref.shape[1]
    cuts = [pl.ds(first, width // CUTS) for first in range(0, width, width // CUTS)]
    pairs = [(texts_hbm, texts_ref), (head_hbm, head_ref), (images_hbm, images_ref)]
    for source, target in ((fc_in_hbm, fc_in_ref), (fc_out_hbm, fc_out_ref)):
        pairs += [(source.at[:, cut], target.at[:, cut]) for cut in cuts]
    copies = [
        pltpu.make_async_copy(source, target, sems.at[index])
        for index, (source, target) in enumerate(pairs)
    ]
    for copy in copies:
        copy.start()
    for copy in copies[:2]:
        copy.wait()
    text_term[...] = dot(texts_ref[...], head_ref[...], 0, 0)
    copies[2].wait()
    pre_act = None
    for cut, copy in zip(cuts, copies[3 : 3 + CUTS]):
        copy.wait()
        part = dot(fc_in_ref[:, cut], images_ref[:, cut], 1, 1)
        pre_act = part if pre_act is None else pre_act + part
    square = pre_act * pre_act
    bent = jnp.tanh(GELU_SCALE * pre_act * (1.0 + GELU_CUBIC * square))
    activation = (0.5 * pre_act * (1.0 + bent)).astype(jnp.bfloat16)
    slope_ref[...] = 0.5 * (1.0 + bent) + (
        0.5 * GELU_SCALE * pre_act * (1.0 - bent * bent) * (1.0 + 3.0 * GELU_CUBIC * square)
    )
    slope_copy = pltpu.make_async_copy(slope_ref, slope_hbm, sems.at[len(copies)])
    slope_copy.start()
    for cut, copy in zip(cuts, copies[3 + CUTS :]):
        copy.wait()
        image_term[:, cut] = dot(activation, fc_out_ref[:, cut], 0, 0)
    for first, term in ((0, image_term), (HALF, text_term)):
        kept_ref[first : first + HALF] = own_half(term, core).astype(jnp.bfloat16)
        sent_ref[first : first + HALF] = own_half(term, 1 - core).astype(jnp.bfloat16)
    slope_copy.wait()


def core_sum_kernel(kept_ref, swapped_ref, own_ref, moved_ref):
    core, side, unused = here()
    got = swapped_ref[1 - core].astype(jnp.float32)
    sums = (kept_ref[...].astype(jnp.float32) + got).astype(jnp.bfloat16)
    own_ref[...] = jnp.where(side == 0, sums[:HALF], sums[HALF:])
    moved_ref[...] = jnp.where(side == 0, sums[HALF:], sums[:HALF])


def embed_rows(chip_ref, other, images_ref, image_side):
    core, side, unused = here()
    residual = own_half(images_ref, core).astype(jnp.float32)
    sums = chip_ref[...].astype(jnp.float32) + other.astype(jnp.float32)
    return sums + jnp.where(side == image_side, residual, 0.0)


def moved_unit_kernel(chip_ref, chips_ref, images_ref, sent_ref):
    other = chips_ref[1 - lax.axis_index("y_hi")]
    rows = embed_rows(chip_ref, other, images_ref, 1)
    inverse = lax.rsqrt(jnp.sum(rows * rows, axis=1, keepdims=True) + epsilon)
    sent_ref[...] = (rows * inverse).astype(jnp.bfloat16)


def own_unit_kernel(chip_ref, other_ref, images_ref, unit_ref, inverse_ref, sent_ref):
    rows = embed_rows(chip_ref, other_ref[...], images_ref, 0)
    inverse = lax.rsqrt(jnp.sum(rows * rows, axis=1, keepdims=True) + epsilon)
    unit_ref[...] = rows * inverse
    inverse_ref[...] = jnp.broadcast_to(inverse, (HALF, LANES))
    sent_ref[...] = (rows * inverse).astype(jnp.bfloat16)


def split_loss(loss):
    high = loss.astype(jnp.bfloat16).astype(jnp.float32)
    lanes = lax.broadcasted_iota(jnp.int32, (loss.shape[0], LANES), 1)
    return jnp.where(lanes == 0, high, jnp.where(lanes == 1, loss - high, 0.0))


def pair_terms(own, others, positive):
    logits = logit_scale * dot(own, others, 1, 1) + logit_bias
    if positive is None:
        flipped = logits
    else:
        flipped = jnp.where(positive, -logits, logits)
    small = jnp.exp(-jnp.abs(flipped))
    loss = jnp.maximum(flipped, 0.0) + jnp.log1p(small)
    sigmoid = jnp.where(flipped >= 0.0, 1.0, small) / (1.0 + small)
    if positive is None:
        pair_grad = loss_scale * sigmoid
    else:
        pair_grad = jnp.where(positive, -loss_scale, loss_scale) * sigmoid
    return logit_scale * dot(pair_grad.astype(jnp.bfloat16), others, 1, 0), loss


def early_kernel(own_ref, first_ref, second_ref, part_ref):
    rows, width = own_ref.shape
    own = own_ref[...]
    first, first_loss = pair_terms(own, first_ref[...], None)
    second, second_loss = pair_terms(own, second_ref[...], None)
    part_ref[:, :width] = first + second
    loss = jnp.sum(first_loss + second_loss, axis=1, keepdims=True)
    part_ref[:, width:] = jnp.broadcast_to(loss, (rows, LANES))


def late_kernel(
    own_ref, moved_ref, third_ref, fourth_ref, column_ref, row_ref, early_ref,
    kept_ref, sent_ref, part_ref,
):
    core, side, unused = here()
    rows, width = own_ref.shape
    own = own_ref[...]
    across = lax.broadcasted_iota(jnp.int32, (rows, rows), 1) == column_ref[...]
    down = lax.broadcasted_iota(jnp.int32, (rows, rows), 0) == row_ref[...]
    paired = jnp.where(side == 0, across.astype(jnp.int32), down.astype(jnp.int32))
    third, third_loss = pair_terms(own, third_ref[...], None)
    last = jnp.where(core == 0, moved_ref[...], fourth_ref[...])
    last, last_loss = pair_terms(own, last, paired == 1)
    part_ref[:, :width] = early_ref[:, :width] + third + last
    loss = jnp.sum(third_loss + last_loss, axis=1, keepdims=True)
    part_ref[:, width:] = split_loss(early_ref[:, width : width + 1] + loss)
    kept_ref[...] = own_half(part_ref, core)
    sent_ref[...] = own_half(part_ref, 1 - core).astype(jnp.bfloat16)


def tangent_kernel(kept_ref, swapped_ref, unit_ref, inverse_ref, sent_ref):
    width = unit_ref.shape[1]
    core, unused, unused = here()
    sums = kept_ref[...] + swapped_ref[1 - core].astype(jnp.float32)
    grad, unit = sums[:, :width], unit_ref[...]
    along = jnp.sum(unit * grad, axis=1, keepdims=True)
    tangent = (grad - unit * along) * inverse_ref[:, :1]
    sent_ref[:, :width] = tangent.astype(jnp.bfloat16)
    loss = sums[:, width : width + 1] + sums[:, width + 1 : width + 2]
    sent_ref[:, width:] = split_loss(loss).astype(jnp.bfloat16)


def backward_kernel(
    grads_ref, slope_ref, fc_out_ref, head_ref, hidden_ref, text_ref, loss_ref
):
    rows, width = 2 * HALF, fc_out_ref.shape[1]
    unused, unused, flip = here()
    image_chip = flip * 2
    image_grad = grads_ref[pl.ds(image_chip, 2)].reshape(rows, width + LANES)
    text_grad = grads_ref[pl.ds(2 - image_chip, 2)].reshape(rows, width + LANES)
    losses = jnp.sum(image_grad[:, width:].astype(jnp.float32), axis=1, keepdims=True)
    loss_ref[...] = jnp.broadcast_to(losses, (rows, LANES)).T[:1] / (WINDOW * rows)
    act_grad = dot(fc_out_ref[...], image_grad[:, :width], 1, 1)
    hidden_ref[...] = (slope_ref[...] * act_grad).astype(jnp.bfloat16)
    text_ref[...] = dot(head_ref[...], text_grad[:, :width], 1, 1).astype(jnp.bfloat16)


def kernel(body, outs, scratch=(), places="", vmem=24, out_places=None):
    spaces = dict(v=pltpu.VMEM, h=pltpu.HBM)
    return pl.pallas_call(
        body,
        out_shape=[jax.ShapeDtypeStruct(shape, dtype) for shape, dtype in outs],
        in_specs=[pl.BlockSpec(memory_space=spaces[place]) for place in places],
        out_specs=[
            pl.BlockSpec(memory_space=spaces[place]) for place in out_places or "v" * len(outs)
        ],
        scratch_shapes=list(scratch),
        compiler_params=pltpu.CompilerParams(vmem_limit_bytes=vmem * 1024 * 1024),
    )


def local(images, texts, fc_in, fc_out, head, partner):
    rows, width = images.shape
    hidden, features = fc_out.shape[0], head.shape[0]
    f32, bf16 = jnp.float32, jnp.bfloat16
    slope, kept, sent = kernel(
        heads_kernel,
        [((hidden, rows), f32), ((rows, width), bf16), ((rows, width), bf16)],
        [
            pltpu.VMEM((hidden, rows), f32),
            pltpu.VMEM((features, rows), bf16),
            pltpu.VMEM((features, width), bf16),
            pltpu.VMEM((rows, width), bf16),
            pltpu.VMEM((hidden, width), bf16),
            pltpu.VMEM((hidden, width), bf16),
            pltpu.VMEM((rows, width), f32),
            pltpu.VMEM((rows, width), f32),
            pltpu.SemaphoreType.DMA((4 + 2 * CUTS,)),
        ],
        "hhhhh",
        vmem=HEADS_VMEM,
        out_places="hvv",
    )(texts.T, head, images, fc_in.T, fc_out)
    half = ((HALF, width), bf16)
    own_chip, moved_chip = kernel(core_sum_kernel, [half, half], places="vv")(
        kept, lax.all_gather(sent, "core")
    )
    moved_other = lax.all_gather(own_chip, "y_hi")
    own_other = lax.ppermute(moved_chip, "y_hi", [(0, 1), (1, 0)])
    (moved_sent,) = kernel(moved_unit_kernel, [half], places="vvv")(
        moved_chip, moved_other, images
    )
    moved = lax.all_gather(moved_sent, "core", tiled=True)
    first = move(moved, FIRST)
    second = move(moved, SECOND)
    unit, inverse, own_sent = kernel(
        own_unit_kernel, [((HALF, width), f32), ((HALF, LANES), f32), half], places="vvv"
    )(own_chip, own_other, images)
    own = lax.all_gather(own_sent, "core", tiled=True)
    third = move(first, (RELAY, RELAY))
    fourth = move(second, (0, RELAY))

    paired = jnp.where(lax.axis_index("core") == 0, partner, -1)
    columns = width + LANES
    part = [((rows, columns), f32)]
    (early,) = kernel(early_kernel, part, places="vvv")(own, first, second)
    kept, sent = kernel(
        late_kernel,
        [((HALF, columns), f32), ((HALF, columns), bf16)],
        [pltpu.VMEM(*part[0])],
        "vvvvvvv",
    )(own, moved, third, fourth, paired.reshape(rows, 1), paired.reshape(1, rows), early)

    (grads,) = kernel(tangent_kernel, [((HALF, columns), bf16)], places="vvvv")(
        kept, lax.all_gather(sent, "core"), unit, inverse
    )
    hidden_grad, text_grad, loss = kernel(
        backward_kernel,
        [((hidden, rows), bf16), ((features, rows), bf16), ((1, rows), f32)],
        places="vvvv",
    )(lax.all_gather(grads, MP), slope, fc_out, head)
    return (hidden_grad.T, text_grad.T, loss.reshape(rows))


def solution(mesh):
    dp = ("z", "y_lo", "x")
    return jax.shard_map(
        local,
        mesh=Mesh(mesh.devices.reshape(SIZES), AXES),
        in_specs=(P(dp, None), P(dp, MP), P(None, MP), P(MP, None), P(MP, None), P(dp)),
        out_specs=(P(dp, MP), P(dp, MP), P(dp)),
        check_vma=False,
    )
```
